32 devices in a mesh: seq: 16 (over z, x, core), exp: 2 (over y).
Axes of the slice: x: 2, y: 2, z: 4, core: 2. Of those that a mesh axis runs over, the one named last changes fastest.
Arguments:
- inner_x: bfloat16 [2048, 8192], P('seq', 'exp'), may hold values from -6 to 6
- inner_z: bfloat16 [2048, 8192], P('seq', 'exp'), may hold values from -6 to 6
- step_raw: bfloat16 [2048, 8192], P('seq', 'exp'), may hold values from -4.5 to 3
- conv_weight: float32 [4, 8192], P(None, 'exp'), may hold values from -3 to 3
- state_proj: bfloat16 [8192, 32], P('exp'), may hold values from -0.125 to 0.125
- step_bias: float32 [8192], P('exp'), may hold values from -7 to -2.3
- decay_log: float32 [16, 8192], P(None, 'exp'), may hold values from -4 to 2.8
- skip_gain: float32 [8192], P('exp'), may hold values from 0.5 to 1.5
- moe_tokens: bfloat16 [2048, 4096], P('seq', 'exp'), may hold values from -6 to 6
- routes: int32 [2048, 2], P('seq'), may hold values from 0 to 15, all different within a row; in each aligned block of 128 rows (0 to 127, 128 to 255, ...) at most 20 rows name the same one
- gate_weight: bfloat16 [2, 12288, 4096], P('exp', 'seq'), may hold values from -0.09375 to 0.09375
- up_weight: bfloat16 [2, 12288, 4096], P('exp', 'seq'), may hold values from -0.09375 to 0.09375
Outputs:
- mixed: bfloat16 [2048, 8192], P('seq', 'exp')
- hidden: bfloat16 [2, 12288, 320], P('exp', 'seq')
The draws below stay inside these ranges and needn't reach their ends.
Inputs may be any that keep to these rules, and one draw needn't show every extreme that they name: `routes`: in each aligned block of 128 rows (the tokens of one device), no expert is named by more than 20 rows, a bound that some block reaches; the two choices of a token differ.
All inputs are finite; a program needn't handle non-finite values.
Results may differ from the reference program's by a relative error of at most 0.0051.
Values may be sent and summed in bfloat16 or wider, within the bound.
A program may use at most 128 MiB of HBM per device.

```python
import math
import jax
import jax.numpy as jnp
import numpy as np
from jax import lax

D = 4096
E = 8192
STATE = 16
CONV = 4
EXPERTS = 16
TOP = 2
FF = 12288
TOK_DEV = 128
CAP = 20
FLIGHT = 2
TOKENS = 2048
N_SEQ = 16


def draw_step_raw(key, part):
    offset_key = jax.random.fold_in(key, 11)
    noise_key = jax.random.fold_in(key, 12)
    offset = jax.random.uniform(offset_key, (E,), jnp.float32, -2.5, 0.0)
    noise = 0.5 * jax.random.normal(noise_key, (TOKENS, E), jnp.float32)
    return jnp.clip(noise + offset[None, :], -4.5, 3.0).astype(jnp.bfloat16)


def block_levels(rng, extent, pieces, least, high):
    def one(position, shards_of):
        heights = jax.random.uniform(jax.random.fold_in(jax.random.fold_in(rng, 6), position), (shards_of,), jnp.float32, least / len(pieces), high / len(pieces))
        return jnp.repeat(jnp.exp(heights), extent[position] // shards_of).reshape((-1,) + (1,) * (len(extent) - position - 1))

    gain = one(*pieces[0])
    for cut in pieces[1:]:
        gain = gain * one(*cut)
    return gain


def deal_out(own_key, own, number, rows, number_of, top, most, lean):
    sequence = jax.random.permutation(own_key, number_of)
    packed, common = shares(number_of, rows * top, most, lean, True), shares(number_of, rows * top, most, lean, False)
    places = jnp.arange(number_of)

    def named(tallies, offset_by):
        used = int((tallies > 0).sum())
        fixed = max(1, used // 4)
        moved = fixed + (places - fixed + offset_by * (used - fixed)) % max(1, number_of - fixed)
        return jnp.zeros((number_of,), jnp.int32).at[sequence[jnp.where(places < fixed, places, moved)]].set(jnp.asarray(tallies, jnp.int32))

    tallies = jnp.where(number % 4 == 0, named(packed, number // 4), named(common, number - number // 4 - 1))
    mixed = jax.random.permutation(jax.random.fold_in(own, 3), number_of)
    source_of, sink = mixed[0:number_of // 2 * 2:2], mixed[1:number_of // 2 * 2:2]
    margin = jnp.minimum(tallies[source_of] - 1, most - tallies[sink]) // 2
    margin = jnp.where((source_of == sequence[0]) | (sink == sequence[0]) | (tallies[sink] == 0), 0, jnp.maximum(margin, 0))
    moved = jax.random.randint(jax.random.fold_in(own, 4), (number_of // 2,), 0, 1 << 20) % (margin + 1)
    tallies = tallies.at[source_of].add(-moved).at[sink].add(moved)
    labels = jnp.searchsorted(jnp.cumsum(tallies), jnp.arange(rows * top), side="right").astype(jnp.int32)
    grid = labels.reshape(top, rows).T
    grid = grid[jax.random.permutation(jax.random.fold_in(own, 1), rows)]
    offset_by = jax.random.randint(jax.random.fold_in(own, 2), (rows, 1), 0, top)
    return jnp.take_along_axis(grid, (jnp.arange(top)[None, :] + offset_by) % top, axis=1)


def shares(count, total, limit, slope, full):
    loads = [(1 << 20) // math.isqrt(standing ** slope) + 1 for standing in range(1, count + 1)]
    largest = limit if full else min(limit, max(-(-total // count), total * loads[0] // sum(loads)))
    least = 1 if total - largest >= count - 1 else 0
    given, spare = [largest] + [least] * (count - 1), total - largest - least * (count - 1)
    while spare > 0:
        free = [i for i in range(1, count) if given[i] < largest] or [i for i in range(1, count) if given[i] < limit]
        pool, budget = sum([loads[i] for i in free]), spare
        for i in free:
            extra = min(limit - given[i], max(1, budget * loads[i] // pool), spare)
            given[i] = given[i] + extra
            spare = spare - extra
    return np.array(given)


def bell_draw(rng, shape, deviation, reach, shards=(), kind=jnp.bfloat16):
    factor_of = block_levels(rng, shape, shards, -0.22, 0.18) if shards else 1.0
    entries = jax.random.normal(rng, shape, jnp.float32) * deviation * factor_of
    return jnp.minimum(jnp.maximum(entries, -reach), reach).astype(kind)


def setup_inputs(seed: int = 0) -> dict:
    key_of = jax.random.split(jax.random.key(seed), 13)
    inner_x = bell_draw(key_of[0], (TOKENS, E), 1.0, 6.0, ((0, 16), (1, 2)))
    inner_z = bell_draw(key_of[1], (TOKENS, E), 1.0, 6.0, ((0, 16), (1, 2)))
    step_raw = draw_step_raw(jax.random.fold_in(key_of[12], 71), 0)
    conv_weight = bell_draw(key_of[3], (CONV, E), CONV ** -0.5, 3.0, ((1, 2),), jnp.float32)
    state_proj = bell_draw(key_of[4], (E, 2 * STATE), (E // 4) ** -0.5, 0.125, ((0, 2),))
    step_bias = jnp.clip(-7.0 + 4.7 * jax.random.uniform(key_of[5], (E,), jnp.float32) ** block_levels(key_of[5], (E,), ((0, 2),), -0.2, 0.2), -7.0, -2.3)
    decay_log = jnp.clip(-4.0 + 6.8 * jax.random.uniform(key_of[6], (STATE, E), jnp.float32) ** block_levels(key_of[6], (STATE, E), ((1, 2),), -0.2, 0.2), -4.0, 2.8)
    skip_gain = jnp.clip(0.5 + 1.0 * jax.random.uniform(key_of[7], (E,), jnp.float32) ** block_levels(key_of[7], (E,), ((0, 2),), -0.2, 0.2), 0.5, 1.5)
    moe_tokens = bell_draw(key_of[8], (TOKENS, D), 1.0, 6.0, ((0, 16), (1, 2)))
    routes_keys = jax.random.split(jax.random.fold_in(key_of[9], 1), TOKENS // TOK_DEV)
    routes_turns = jax.random.permutation(jax.random.fold_in(key_of[9], 3), TOKENS // TOK_DEV)
    routes = jax.vmap(lambda own, number: deal_out(jax.random.fold_in(key_of[9], 2), own, number, TOK_DEV, EXPERTS, TOP, CAP, 2))(routes_keys, routes_turns).reshape((TOKENS, TOP))
    gate_weight = bell_draw(key_of[10], (FLIGHT, FF, D), D ** -0.5, 0.09375, ((0, 2), (1, 16)))
    up_weight = bell_draw(key_of[11], (FLIGHT, FF, D), D ** -0.5, 0.09375, ((0, 2), (1, 16)))
    return dict(inner_x=inner_x, inner_z=inner_z, step_raw=step_raw, conv_weight=conv_weight, state_proj=state_proj, step_bias=step_bias, decay_log=decay_log, skip_gain=skip_gain, moe_tokens=moe_tokens, routes=routes, gate_weight=gate_weight, up_weight=up_weight)


def expand_rows(slot_rows, gate_matrix, up_matrix):
    dims = (((1,), (1,)), ((), ()))
    gate_part = lax.dot_general(gate_matrix, slot_rows, dims, preferred_element_type=jnp.float32)
    up_part = lax.dot_general(up_matrix, slot_rows, dims, preferred_element_type=jnp.float32)
    return (jax.nn.silu(gate_part) * up_part).astype(jnp.bfloat16)


def slot_table(pair_ids, experts_count, capacity, tokens):
    onehot = (pair_ids[:, None] == jnp.arange(experts_count, dtype=jnp.int32)[None, :]).astype(jnp.int32)
    before = jnp.cumsum(onehot, axis=0) - onehot
    places = (before[:, :, None] == jnp.arange(capacity, dtype=jnp.int32)[None, None, :]).astype(jnp.int32)
    chosen = onehot[:, :, None] * places
    return jnp.sum(chosen.reshape(tokens, -1, experts_count * capacity), axis=1)


def mixer(inner_x, inner_z, step_raw, conv_weight, state_proj, step_bias, decay_log, skip_gain):
    length = inner_x.shape[0]
    taps = conv_weight.shape[0]
    widened = inner_x.astype(jnp.float32)
    padded = jnp.concatenate([jnp.zeros((taps - 1, widened.shape[1]), jnp.float32), widened], axis=0)
    conv_sum = jnp.zeros(widened.shape, jnp.float32)
    for offset in range(taps):
        conv_sum = conv_sum + conv_weight[offset][None, :] * padded[offset:offset + length]
    conv_out = jax.nn.silu(conv_sum)
    coeffs = jnp.dot(conv_out.astype(jnp.bfloat16), state_proj, preferred_element_type=jnp.float32)
    input_coef = coeffs[:, :STATE]
    output_coef = coeffs[:, STATE:]
    step_size = jax.nn.softplus(step_raw.astype(jnp.float32) + step_bias[None, :])
    rates = -jnp.exp(decay_log)

    def advance(state, row):
        step_row, in_row, out_row, conv_row = row
        state = jnp.exp(rates * step_row[None, :]) * state + in_row[:, None] * (step_row * conv_row)[None, :]
        return state, jnp.sum(out_row[:, None] * state, axis=0)

    start_state = jnp.zeros(rates.shape, jnp.float32)
    _, outputs = lax.scan(advance, start_state, (step_size, input_coef, output_coef, conv_out))
    result = (outputs + skip_gain[None, :] * conv_out) * jax.nn.silu(inner_z.astype(jnp.float32))
    return result.astype(jnp.bfloat16)


def expert_layer(moe_tokens, routes, gate_weight, up_weight):
    flight = gate_weight.shape[0]
    block_ids = routes.reshape(N_SEQ, TOK_DEV * TOP)
    block_rows = moe_tokens.reshape(N_SEQ, TOK_DEV, D)

    def dispatch(args):
        pair_ids, token_rows = args
        table = slot_table(pair_ids, flight, CAP, TOK_DEV)
        return jnp.dot(table.T.astype(jnp.bfloat16), token_rows, preferred_element_type=jnp.float32).astype(jnp.bfloat16)

    placed = lax.map(dispatch, (block_ids, block_rows))
    placed = placed.reshape(N_SEQ, flight, CAP, D).transpose(1, 0, 2, 3).reshape(flight, N_SEQ * CAP, D)

    def per_expert(args):
        slot_rows, gate_matrix, up_matrix = args
        return expand_rows(slot_rows, gate_matrix, up_matrix)

    return lax.map(per_expert, (placed, gate_weight, up_weight))


def reference(inner_x, inner_z, step_raw, conv_weight, state_proj, step_bias, decay_log, skip_gain, moe_tokens, routes, gate_weight, up_weight):
    mixed = mixer(inner_x, inner_z, step_raw, conv_weight, state_proj, step_bias, decay_log, skip_gain)
    hidden = expert_layer(moe_tokens, routes, gate_weight, up_weight)
    return (mixed, hidden)
```

```python
import functools

import jax
import jax.numpy as jnp
from jax import lax
from jax.experimental import pallas as pl
from jax.experimental.pallas import tpu as pltpu
from jax.sharding import PartitionSpec as P

CAP = 20
LANES = 128
SUB = 8
LOG2E = 1.4426950408889634
MESH = pl.DeviceIdType.MESH
VMEM_LIMIT = 48 * 1024 * 1024


def silu(value):
    half = 0.5 * value
    return half + half * jnp.tanh(half)


def softplus(value):
    grown = jnp.exp(value)
    series = grown * (1.0 - grown * (0.5 - grown * (1.0 / 3.0 - 0.25 * grown)))
    return jnp.where(grown < 0.03, series, jnp.log(1.0 + grown))


def front_kernel(
    x_ref, rim_ref, raw_ref, taps_ref, proj_ref, bias_ref, conv_ref, step_ref, drive_ref, coef_ref, wide, rounded
):
    length, channels = x_ref.shape
    taps = taps_ref.shape[0]

    def tile(position, carry):
        lanes = pl.ds(pl.multiple_of(position * LANES, LANES), LANES)
        rows = pl.ds(pl.multiple_of(position * length, length), length)
        wide[pl.ds(0, 16), :] = rim_ref[:, lanes].astype(jnp.float32)
        wide[pl.ds(16, length), :] = x_ref[:, lanes].astype(jnp.float32)
        total = taps_ref[pl.ds(0, 1), lanes] * wide[pl.ds(17 - taps, length), :]
        for tap in range(1, taps):
            total = total + taps_ref[pl.ds(tap, 1), lanes] * wide[pl.ds(17 - taps + tap, length), :]
        conv = silu(total)
        step = softplus(raw_ref[:, lanes].astype(jnp.float32) + bias_ref[:, lanes])
        conv_ref[rows, :] = conv
        step_ref[rows, :] = step
        drive_ref[rows, :] = step * conv
        rounded[:, lanes] = conv.astype(jnp.bfloat16)
        return carry

    lax.fori_loop(0, channels // LANES, tile, 0)
    coef_ref[...] = jnp.dot(rounded[...], proj_ref[...], preferred_element_type=jnp.float32)


def splat_columns(coef_ref, first, count, table):
    length = coef_ref.shape[0]
    for column in range(count):
        table[pl.ds(column * length, length), :] = jnp.broadcast_to(
            coef_ref[:, first + column : first + column + 1], (length, LANES)
        )


def rate_rows(decay_ref, table):
    states, channels = decay_ref.shape

    def tile(position, carry):
        lanes = pl.ds(pl.multiple_of(position * LANES, LANES), LANES)
        rows = pl.ds(pl.multiple_of(position * states, states), states)
        table[rows, :] = jnp.exp(decay_ref[:, lanes]) * (-LOG2E)
        return carry

    lax.fori_loop(0, channels // LANES, tile, 0)


def first_kernel(step_ref, drive_ref, coef_ref, decay_ref, end_ref, total_ref, rate_ref, in_table):
    states, channels = decay_ref.shape
    length = coef_ref.shape[0]
    groups = channels // (LANES * SUB)
    splat_columns(coef_ref, 0, states, in_table)
    rate_rows(decay_ref, rate_ref)

    def group(position, carry):
        base = position * SUB
        rates = [rate_ref[pl.ds(base * states + n, SUB, stride=states), :] for n in range(states)]

        def block(turn, held):
            total, state = held[0], list(held[1:])
            for inner in range(4):
                t = turn * 4 + inner
                step = step_ref[pl.ds(base * length + t, SUB, stride=length), :]
                drive = drive_ref[pl.ds(base * length + t, SUB, stride=length), :]
                total = total + step
                for n in range(states):
                    row = in_table[pl.ds(n * length + t, 1), :]
                    state[n] = jnp.exp2(rates[n] * step) * state[n] + row * drive
            return (total, *state)

        zero = jnp.zeros((SUB, LANES), jnp.float32)
        held = lax.fori_loop(0, length // 4, block, (zero,) * (states + 1))
        total_ref[pl.ds(pl.multiple_of(base, SUB), SUB), :] = held[0]
        for n in range(states):
            end_ref[pl.ds(base * states + n, SUB, stride=states), :] = held[1 + n]
        return carry

    lax.fori_loop(0, groups, group, 0)


def second_kernel(
    step_ref, drive_ref, conv_ref, z_ref, coef_ref, rate_ref, start_ref, gain_ref, mixed_ref, in_table, out_table, sums
):
    length, channels = z_ref.shape
    states = coef_ref.shape[1] // 2
    groups = channels // (LANES * SUB)
    splat_columns(coef_ref, 0, states, in_table)
    splat_columns(coef_ref, states, states, out_table)

    def group(position, carry):
        base = position * SUB
        rates = [rate_ref[pl.ds(base * states + n, SUB, stride=states), :] for n in range(states)]
        start = tuple(
            start_ref[pl.ds(base * states + n, SUB, stride=states), :] for n in range(states)
        )

        def block(turn, held):
            state = list(held)
            for inner in range(4):
                t = turn * 4 + inner
                step = step_ref[pl.ds(base * length + t, SUB, stride=length), :]
                drive = drive_ref[pl.ds(base * length + t, SUB, stride=length), :]
                parts = [None, None]
                for n in range(states):
                    row = in_table[pl.ds(n * length + t, 1), :]
                    state[n] = jnp.exp2(rates[n] * step) * state[n] + row * drive
                    term = out_table[pl.ds(n * length + t, 1), :] * state[n]
                    parts[n % 2] = term if parts[n % 2] is None else parts[n % 2] + term
                sums[pl.ds(base * length + t, SUB, stride=length), :] = parts[0] + parts[1]
            return tuple(state)

        lax.fori_loop(0, length // 4, block, start)
        return carry

    lax.fori_loop(0, groups, group, 0)

    def tile(position, carry):
        lanes = pl.ds(pl.multiple_of(position * LANES, LANES), LANES)
        rows = pl.ds(pl.multiple_of(position * length, length), length)
        result = sums[rows, :] + gain_ref[:, lanes] * conv_ref[rows, :]
        mixed_ref[:, lanes] = (result * silu(z_ref[:, lanes].astype(jnp.float32))).astype(jnp.bfloat16)
        return carry

    lax.fori_loop(0, channels // LANES, tile, 0)


def carry_kernel(
    count, end_ref, total_ref, rate_ref, start_ref, got_end, got_total, leaving, sends, arrivals
):
    me, side = lax.axis_index("seq"), lax.axis_index("exp")
    piece = end_ref.shape[1]

    def peer_of(distance):
        return lax.rem(me + distance, count)

    barrier = pltpu.get_barrier_semaphore()

    def greet(distance, carry):
        pl.semaphore_signal(barrier, inc=1, device_id=(peer_of(distance), side), device_id_type=MESH)
        return carry

    lax.fori_loop(1, count, greet, 0)
    pl.semaphore_wait(barrier, count - 1)

    def end_copy(distance):
        peer = peer_of(distance)
        return pltpu.make_async_remote_copy(
            end_ref.at[peer], got_end.at[me], sends.at[0, distance], arrivals.at[0, distance],
            device_id=(peer, side), device_id_type=MESH,
        )

    def total_copy(distance):
        peer = peer_of(distance)
        return pltpu.make_async_remote_copy(
            total_ref.at[peer], got_total.at[me], sends.at[1, distance], arrivals.at[1, distance],
            device_id=(peer, side), device_id_type=MESH,
        )

    def back_copy(distance):
        peer = peer_of(distance)
        return pltpu.make_async_remote_copy(
            leaving.at[peer], start_ref.at[me], sends.at[2, distance], arrivals.at[2, distance],
            device_id=(peer, side), device_id_type=MESH,
        )

    def send(distance, carry):
        end_copy(distance).start()
        total_copy(distance).start()
        return carry

    lax.fori_loop(1, count, send, 0)
    got_end[me] = end_ref[me]
    got_total[me] = total_ref[me]

    def receive(distance, carry):
        end_copy(distance).wait()
        total_copy(distance).wait()
        return carry

    lax.fori_loop(1, count, receive, 0)
    rates = rate_ref[me]
    spread = got_total.shape[1]

    def join(source, state):
        leaving[source] = state.astype(jnp.bfloat16)
        totals = got_total[source]
        totals = jnp.broadcast_to(totals[:, None, :], (spread, piece // spread, LANES)).reshape(piece, LANES)
        return jnp.exp2(rates * totals) * state + got_end[source].astype(jnp.float32)

    lax.fori_loop(0, count, join, jnp.zeros((piece, LANES), jnp.float32))

    def send_back(distance, carry):
        back_copy(distance).start()
        return carry

    lax.fori_loop(1, count, send_back, 0)
    start_ref[me] = leaving[me]

    def receive_back(distance, carry):
        back_copy(distance).wait()
        return carry

    lax.fori_loop(1, count, receive_back, 0)


def expand_rows(slot_rows, gate_matrix, up_matrix):
    dims = (((1,), (1,)), ((), ()))
    gate_part = lax.dot_general(gate_matrix, slot_rows, dims, preferred_element_type=jnp.float32)
    up_part = lax.dot_general(up_matrix, slot_rows, dims, preferred_element_type=jnp.float32)
    return (jax.nn.silu(gate_part) * up_part).astype(jnp.bfloat16)


def slot_table(pair_ids, experts_count, capacity, tokens):
    onehot = (pair_ids[:, None] == jnp.arange(experts_count, dtype=jnp.int32)[None, :]).astype(
        jnp.int32
    )
    before = jnp.cumsum(onehot, axis=0) - onehot
    places = (before[:, :, None] == jnp.arange(capacity, dtype=jnp.int32)[None, None, :]).astype(
        jnp.int32
    )
    chosen = onehot[:, :, None] * places
    return jnp.sum(chosen.reshape(tokens, -1, experts_count * capacity), axis=1)


def f32(*shape):
    return jax.ShapeDtypeStruct(shape, jnp.float32)


def kernel_call(body, outs, scratch, **params):
    return pl.pallas_call(
        body,
        out_shape=outs,
        scratch_shapes=scratch,
        compiler_params=pltpu.CompilerParams(vmem_limit_bytes=VMEM_LIMIT, **params),
    )


def shards(
    inner_x,
    inner_z,
    step_raw,
    conv_weight,
    state_proj,
    step_bias,
    decay_log,
    skip_gain,
    moe_tokens,
    routes,
    gate_weight,
    up_weight,
):
    length, channels = inner_x.shape
    states = decay_log.shape[0]
    count, flight = lax.axis_size("seq"), lax.axis_size("exp")
    rim = lax.ppermute(inner_x[length - 16 :], "seq", [(s, s + 1) for s in range(count - 1)])
    table = slot_table(routes.reshape(-1), flight, CAP, routes.shape[0])
    placed = jnp.dot(
        table.T.astype(jnp.bfloat16), moe_tokens, preferred_element_type=jnp.float32
    ).astype(jnp.bfloat16)
    placed = placed.reshape(flight, CAP, moe_tokens.shape[1])
    arrived = lax.all_to_all(placed, "exp", split_axis=0, concat_axis=2, tiled=True)
    slot_rows = lax.all_gather(arrived[0], "seq", axis=0, tiled=True)

    tiles = channels // LANES
    flat = f32(tiles * length, LANES)
    conv, step, drive, partial_coef = kernel_call(
        front_kernel,
        (flat, flat, flat, f32(length, 2 * states)),
        [pltpu.VMEM((length + 16, LANES), jnp.float32), pltpu.VMEM((length, channels), jnp.bfloat16)],
    )(inner_x, rim, step_raw, conv_weight, state_proj, step_bias[None, :])
    coeffs = lax.psum(partial_coef, "exp")
    wide_table = pltpu.VMEM((states * length, LANES), jnp.float32)
    end, total, rates = kernel_call(
        first_kernel,
        (f32(tiles * states, LANES), f32(tiles, LANES), f32(tiles * states, LANES)),
        [wide_table],
    )(step, drive, coeffs, decay_log)
    piece = tiles * states // count
    spread = max(1, piece // states)
    share = max(1, states // piece)
    totals = jnp.broadcast_to(
        total.reshape(tiles // spread, 1, spread, LANES), (tiles // spread, share, spread, LANES)
    ).reshape(count, spread, LANES)
    pieces = (count, piece, LANES)
    start = kernel_call(
        functools.partial(carry_kernel, count),
        jax.ShapeDtypeStruct(pieces, jnp.bfloat16),
        [
            pltpu.VMEM(pieces, jnp.bfloat16),
            pltpu.VMEM(totals.shape, jnp.float32),
            pltpu.VMEM(pieces, jnp.bfloat16),
            pltpu.SemaphoreType.DMA((3, count)),
            pltpu.SemaphoreType.DMA((3, count)),
        ],
        collective_id=0,
        has_side_effects=True,
    )(end.astype(jnp.bfloat16).reshape(pieces), totals, rates.reshape(pieces))
    mixed = kernel_call(
        second_kernel,
        jax.ShapeDtypeStruct((length, channels), jnp.bfloat16),
        [wide_table, wide_table, pltpu.VMEM((tiles * length, LANES), jnp.float32)],
    )(
        step, drive, conv, inner_z, coeffs, rates,
        start.astype(jnp.float32).reshape(tiles * states, LANES), skip_gain[None, :],
    )
    hidden = expand_rows(slot_rows, gate_weight[0], up_weight[0])[None]
    return (mixed, hidden)


def solution(mesh):
    return jax.shard_map(
        shards,
        mesh=mesh,
        in_specs=(
            P("seq", "exp"),
            P("seq", "exp"),
            P("seq", "exp"),
            P(None, "exp"),
            P("exp", None),
            P("exp"),
            P(None, "exp"),
            P("exp"),
            P("seq", "exp"),
            P("seq", None),
            P("exp", "seq", None),
            P("exp", "seq", None),
        ),
        out_specs=(P("seq", "exp"), P("exp", "seq", None)),
        check_vma=False,
    )
```

```python
import functools

import jax
import jax.numpy as jnp
from jax import lax
from jax.experimental import pallas as pl
from jax.experimental.pallas import tpu as pltpu
from jax.sharding import PartitionSpec as P

CAP = 20
LANES = 128
SUB = 8
LOG2E = 1.4426950408889634
MESH = pl.DeviceIdType.MESH
VMEM_LIMIT = 48 * 1024 * 1024


def silu(value):
    half = 0.5 * value
    return half + half * jnp.tanh(half)


def softplus(value):
    grown = jnp.exp(value)
    series = grown * (1.0 - grown * (0.5 - grown * (1.0 / 3.0 - 0.25 * grown)))
    return jnp.where(grown < 0.03, series, jnp.log(1.0 + grown))


def splat_columns(coef_ref, first, count, table):
    length = coef_ref.shape[0]
    for column in range(count):
        table[pl.ds(column * length, length), :] = jnp.broadcast_to(
            coef_ref[:, first + column : first + column + 1], (length, LANES)
        )


def rate_rows(decay_ref, table):
    states, channels = decay_ref.shape

    def tile(position, carry):
        lanes = pl.ds(pl.multiple_of(position * LANES, LANES), LANES)
        rows = pl.ds(pl.multiple_of(position * states, states), states)
        table[rows, :] = jnp.exp(decay_ref[:, lanes]) * (-LOG2E)
        return carry

    lax.fori_loop(0, channels // LANES, tile, 0)


def mixer_kernel(
    count, flight, x_ref, z_ref, raw_ref, taps_ref, proj_ref, bias_ref, decay_ref, gain_ref, tokens_ref, routes_ref,
    gate_hbm, up_hbm, mixed_ref, hidden_ref,
    gate_ref, up_ref, rim_ref, wide, rounded, conv_ref, step_ref, drive_ref, parts_ref, coef_ref, in_table, out_table,
    rate_ref, end_ref, total_ref, end_out, total_out, got_end, got_total, leaving, entering, start_ref, sums,
    stage, block_rows, rows_ref, order_ref,
    local_sem, rim_sem, pair_out, pair_in, rows_out, rows_in, sends, arrivals,
):
    length, channels = x_ref.shape
    states = decay_ref.shape[0]
    taps = taps_ref.shape[0]
    width = tokens_ref.shape[1]
    quarter = width // 4
    tiles = channels // LANES
    piece = tiles * states // count
    spread = got_total.shape[1]
    hidden_rows = gate_ref.shape[0]
    chunk = 256 if hidden_rows % 256 == 0 else hidden_rows
    me, side = lax.axis_index("seq"), lax.axis_index("exp")

    def seq_peer(distance):
        return lax.rem(me + distance, count)

    def exp_peer(distance):
        return lax.rem(side + distance, flight)

    gate_load = pltpu.make_async_copy(gate_hbm, gate_ref, local_sem.at[0])
    up_load = pltpu.make_async_copy(up_hbm, up_ref, local_sem.at[1])
    gate_load.start()
    up_load.start()

    barrier = pltpu.get_barrier_semaphore()

    def greet(distance, carry):
        pl.semaphore_signal(barrier, inc=1, device_id=(seq_peer(distance), side), device_id_type=MESH)
        return carry

    lax.fori_loop(1, count, greet, 0)
    for distance in range(1, flight):
        pl.semaphore_signal(barrier, inc=1, device_id=(me, exp_peer(distance)), device_id_type=MESH)
    pl.semaphore_wait(barrier, count - 1 + flight - 1)

    def remote(source, target, send_sem, arrive_sem, seq_index, exp_index):
        return pltpu.make_async_remote_copy(
            source, target, send_sem, arrive_sem, device_id=(seq_index, exp_index), device_id_type=MESH
        )

    rim_copy = remote(
        x_ref.at[pl.ds(length - 16, 16), :], rim_ref, rim_sem.at[0], rim_sem.at[1], seq_peer(1), side
    )

    @pl.when(me < count - 1)
    def _():
        rim_copy.start()

    above = lax.broadcasted_iota(jnp.int32, (length, length), 0) < lax.broadcasted_iota(
        jnp.int32, (length, length), 1
    )
    above = above.astype(jnp.float32).astype(jnp.bfloat16)
    slot = lax.broadcasted_iota(jnp.int32, (16, length), 0)
    for expert in range(flight):
        named = (routes_ref[pl.ds(0, 1), :] == expert).astype(jnp.float32)
        for choice in range(1, routes_ref.shape[0]):
            named = named + (routes_ref[pl.ds(choice, 1), :] == expert).astype(jnp.float32)
        named = jnp.broadcast_to(named, (16, length))
        rank = jnp.dot(named.astype(jnp.bfloat16), above, preferred_element_type=jnp.float32)
        taken = jnp.where(rank == slot.astype(jnp.float32), named, 0.0).astype(jnp.bfloat16)
        stage[expert, :, pl.ds(0, width)] = jnp.dot(
            taken, tokens_ref[...], preferred_element_type=jnp.float32
        ).astype(jnp.bfloat16)
        late = jnp.where(rank == (16 + (slot & 3)).astype(jnp.float32), named, 0.0)
        rest = jnp.zeros((16, quarter), jnp.float32)
        for part in range(4):
            mine = jnp.where((slot >> 2) == part, late, 0.0).astype(jnp.bfloat16)
            rest = rest + jnp.dot(
                mine, tokens_ref[:, pl.ds(part * quarter, quarter)], preferred_element_type=jnp.float32
            )
        stage[expert, :, pl.ds(width, quarter)] = rest.astype(jnp.bfloat16)

    def stage_copy(distance):
        return remote(
            stage.at[exp_peer(distance)], block_rows.at[me, side],
            pair_out.at[0, distance], pair_in.at[0, distance], me, exp_peer(distance),
        )

    def coef_copy(distance):
        return remote(
            parts_ref.at[side], parts_ref.at[side],
            pair_out.at[1, distance], pair_in.at[1, distance], me, exp_peer(distance),
        )

    for distance in range(1, flight):
        stage_copy(distance).start()
    block_rows[me, side] = stage[side]

    def step_tile(position, carry):
        lanes = pl.ds(pl.multiple_of(position * LANES, LANES), LANES)
        rows = pl.ds(pl.multiple_of(position * length, length), length)
        step_ref[rows, :] = softplus(raw_ref[:, lanes].astype(jnp.float32) + bias_ref[:, lanes])
        return carry

    lax.fori_loop(0, tiles, step_tile, 0)
    rate_rows(decay_ref, rate_ref)

    low = lax.rem(me, 4)
    plane = me // 4
    planes = count // 4
    across = me - low + lax.rem(low + 2, 4)
    beside = me + 1 - 2 * lax.rem(me, 2)
    far = across + 1 - 2 * lax.rem(across, 2)

    def row_copy(kind, source):
        target = (me + 4, me - 4, across, beside)[kind]
        return remote(
            block_rows.at[source], block_rows.at[source], rows_out.at[kind, source], rows_in.at[source], target, side
        )

    def arrived(source):
        row_copy(3, source).wait_recv()

    def pass_on(source, up, down, act):
        if up:
            pl.when(plane < planes - 1)(lambda: act(row_copy(0, source)))
        if down:
            pl.when(plane > 0)(lambda: act(row_copy(1, source)))
        act(row_copy(2, source))
        act(row_copy(3, source))

    def column_step(hop, act, wait):
        @pl.when(plane >= hop)
        def _():
            if wait:
                arrived(me - 4 * hop)
            pass_on(me - 4 * hop, True, False, act)

        @pl.when(plane + hop < planes)
        def _():
            if wait:
                arrived(me + 4 * hop)
            pass_on(me + 4 * hop, False, True, act)

    def across_step(hop, act, wait):
        if hop == 0:
            if wait:
                arrived(across)
            act(row_copy(3, across))
            return

        @pl.when(plane >= hop)
        def _():
            if wait:
                arrived(across - 4 * hop)
            act(row_copy(3, across - 4 * hop))

        @pl.when(plane + hop < planes)
        def _():
            if wait:
                arrived(across + 4 * hop)
            act(row_copy(3, across + 4 * hop))

    def start(copy):
        copy.start()

    def sent(copy):
        copy.wait_send()

    for distance in range(1, flight):
        stage_copy(distance).wait()
    pass_on(me, True, True, start)

    @pl.when(me > 0)
    def _():
        rim_copy.wait_recv()

    @pl.when(me == 0)
    def _():
        rim_ref[...] = jnp.zeros_like(rim_ref)

    def conv_tile(position, carry):
        lanes = pl.ds(pl.multiple_of(position * LANES, LANES), LANES)
        rows = pl.ds(pl.multiple_of(position * length, length), length)
        wide[pl.ds(0, 16), :] = rim_ref[:, lanes].astype(jnp.float32)
        wide[pl.ds(16, length), :] = x_ref[:, lanes].astype(jnp.float32)
        total = taps_ref[pl.ds(0, 1), lanes] * wide[pl.ds(17 - taps, length), :]
        for tap in range(1, taps):
            total = total + taps_ref[pl.ds(tap, 1), lanes] * wide[pl.ds(17 - taps + tap, length), :]
        conv = silu(total)
        conv_ref[rows, :] = conv
        drive_ref[rows, :] = step_ref[rows, :] * conv
        rounded[:, lanes] = conv.astype(jnp.bfloat16)
        return carry

    lax.fori_loop(0, tiles, conv_tile, 0)
    parts_ref[side] = jnp.dot(rounded[...], proj_ref[...], preferred_element_type=jnp.float32)
    for distance in range(1, flight):
        coef_copy(distance).start()
    if planes > 1:
        column_step(1, start, True)
    for distance in range(1, flight):
        coef_copy(distance).wait()
    coef = parts_ref[0]
    for other in range(1, flight):
        coef = coef + parts_ref[other]
    coef_ref[...] = coef
    splat_columns(coef_ref, 0, states, in_table)
    splat_columns(coef_ref, states, states, out_table)

    groups = tiles // SUB
    pair = 2 if groups % 2 == 0 else 1
    span = states // pair

    def lines(ref, group, offset, stride):
        return ref[pl.ds(group * SUB * stride + offset, SUB, stride=stride), :]

    def sweep(first, lead, begin, output):
        rates = [[lines(rate_ref, first + g, lead + n, states) for n in range(span)] for g in range(pair)]
        keep_total = lead == 0 and not output

        def block(turn, held):
            state = [list(held[g * span : (g + 1) * span]) for g in range(pair)]
            totals = list(held[pair * span :])
            for inner in range(4):
                t = turn * 4 + inner
                steps = [lines(step_ref, first + g, t, length) for g in range(pair)]
                drives = [lines(drive_ref, first + g, t, length) for g in range(pair)]
                if keep_total:
                    totals = [totals[g] + steps[g] for g in range(pair)]
                terms = [[None, None] for _ in range(pair)]
                for n in range(span):
                    row = in_table[pl.ds((lead + n) * length + t, 1), :]
                    if output:
                        out_row = out_table[pl.ds((lead + n) * length + t, 1), :]
                    for g in range(pair):
                        state[g][n] = jnp.exp2(rates[g][n] * steps[g]) * state[g][n] + row * drives[g]
                        if output:
                            term = out_row * state[g][n]
                            old = terms[g][n % 2]
                            terms[g][n % 2] = term if old is None else old + term
                if output:
                    for g in range(pair):
                        where = pl.ds((first + g) * SUB * length + t, SUB, stride=length)
                        part = terms[g][0] if span == 1 else terms[g][0] + terms[g][1]
                        sums[where, :] = part if lead == 0 else sums[where, :] + part
            return tuple(s for line in state for s in line) + tuple(totals)

        zeros = (jnp.zeros((SUB, LANES), jnp.float32),) * (pair if keep_total else 0)
        held = lax.fori_loop(0, length // 4, block, tuple(begin) + zeros)
        if keep_total:
            for g in range(pair):
                total_ref[pl.ds(pl.multiple_of((first + g) * SUB, SUB), SUB), :] = held[pair * span + g]
        return held

    events = [lambda hop=hop: column_step(hop, start, True) for hop in range(2, planes)]
    events += [lambda hop=hop: across_step(hop, start, True) for hop in range(planes)]
    units = [(first, lead) for first in range(0, groups, pair) for lead in range(0, states, span)]
    for number, (first, lead) in enumerate(units):
        zero = jnp.zeros((SUB, LANES), jnp.float32)
        held = sweep(first, lead, (zero,) * (pair * span), False)
        for g in range(pair):
            for n in range(span):
                end_ref[pl.ds((first + g) * SUB * states + lead + n, SUB, stride=states), :] = held[g * span + n]
        last = number == len(units) - 1
        for _ in range(len(events) if last else min(len(events), -(-planes // 2))):
            events.pop(0)()

    def lay_out(peer, carry):
        end_out[peer] = end_ref[pl.ds(peer * piece, piece), :].astype(jnp.bfloat16)
        total_out[peer] = total_ref[pl.ds(peer * piece // states, spread), :]
        return carry

    lax.fori_loop(0, count, lay_out, 0)

    def carry_copy(kind, distance):
        peer = seq_peer(distance)
        source = (end_out.at[peer], total_out.at[peer], leaving.at[peer])[kind]
        target = (got_end.at[me], got_total.at[me], entering.at[me])[kind]
        return remote(source, target, sends.at[kind, distance], arrivals.at[kind, distance], peer, side)

    def send_ends(distance, carry):
        carry_copy(0, distance).start()
        carry_copy(1, distance).start()
        return carry

    lax.fori_loop(1, count, send_ends, 0)
    got_end[me] = end_out[me]
    got_total[me] = total_out[me]

    def last_rows(turn, carry):
        arrived(lax.rem(beside, 4) + 4 * turn)
        arrived(lax.rem(far, 4) + 4 * turn)
        return carry

    lax.fori_loop(0, planes, last_rows, 0)

    small = 4 * count
    for half in range(flight):
        def lay_rows(source, carry):
            rows_ref[pl.ds(pl.multiple_of(source * 16, 16), 16), pl.ds(half * width, width)] = block_rows[
                source, half, :, pl.ds(0, width)
            ]
            return carry

        lax.fori_loop(0, count, lay_rows, 0)
        rest = block_rows[:, half, :, pl.ds(width, quarter)].reshape(16 * count, quarter)
        into = lax.broadcasted_iota(jnp.int32, (small, 16 * count), 0)
        out_of = lax.broadcasted_iota(jnp.int32, (small, 16 * count), 1)
        for part in range(4):
            pick = ((into >> 2) * 16 + part * 4 + (into & 3) == out_of).astype(jnp.float32).astype(jnp.bfloat16)
            rows_ref[pl.ds(16 * count, small), pl.ds(half * width + part * quarter, quarter)] = jnp.dot(
                pick, rest, preferred_element_type=jnp.float32
            ).astype(jnp.bfloat16)
    held_at = lax.broadcasted_iota(jnp.int32, order_ref.shape, 0)
    wanted = lax.broadcasted_iota(jnp.int32, order_ref.shape, 1)
    tail_at = held_at - 16 * count
    goes_to = jnp.where(
        held_at < 16 * count,
        (held_at >> 4) * CAP + (held_at & 15),
        (tail_at >> 2) * CAP + 16 + (tail_at & 3),
    )
    order_ref[...] = (goes_to == wanted).astype(jnp.float32).astype(jnp.bfloat16)
    gate_load.wait()
    up_load.wait()

    def expand(turn, carry):
        part = pl.ds(pl.multiple_of(turn * chunk, chunk), chunk)
        dims = (((1,), (1,)), ((), ()))
        gate = lax.dot_general(gate_ref[part, :], rows_ref[...], dims, preferred_element_type=jnp.float32)
        up = lax.dot_general(up_ref[part, :], rows_ref[...], dims, preferred_element_type=jnp.float32)
        value = (silu(gate) * up).astype(jnp.bfloat16)
        hidden_ref[part, :] = jnp.dot(value, order_ref[...], preferred_element_type=jnp.float32).astype(
            jnp.bfloat16
        )
        return carry

    turns = hidden_rows // chunk
    lax.fori_loop(0, turns // 2, expand, 0)

    def receive(distance, carry):
        carry_copy(0, distance).wait()
        carry_copy(1, distance).wait()
        return carry

    lax.fori_loop(1, count, receive, 0)
    own_rates = rate_ref[pl.ds(me * piece, piece), :]

    def join(source, state):
        leaving[source] = state.astype(jnp.bfloat16)
        totals = got_total[source]
        totals = jnp.broadcast_to(totals[:, None, :], (spread, piece // spread, LANES)).reshape(piece, LANES)
        return jnp.exp2(own_rates * totals) * state + got_end[source].astype(jnp.float32)

    lax.fori_loop(0, count, join, jnp.zeros((piece, LANES), jnp.float32))

    def send_back(distance, carry):
        carry_copy(2, distance).start()
        return carry

    lax.fori_loop(1, count, send_back, 0)
    entering[me] = leaving[me]
    lax.fori_loop(turns // 2, turns, expand, 0)

    def receive_back(distance, carry):
        carry_copy(2, distance).wait()
        return carry

    lax.fori_loop(1, count, receive_back, 0)

    def widen(source, carry):
        start_ref[pl.ds(source * piece, piece), :] = entering[source].astype(jnp.float32)
        return carry

    lax.fori_loop(0, count, widen, 0)

    def second(turn, carry):
        first = turn * pair
        for lead in range(0, states, span):
            begin = [lines(start_ref, first + g, lead + n, states) for g in range(pair) for n in range(span)]
            sweep(first, lead, begin, True)
        return carry

    lax.fori_loop(0, groups // pair, second, 0)

    def out_tile(position, carry):
        lanes = pl.ds(pl.multiple_of(position * LANES, LANES), LANES)
        rows = pl.ds(pl.multiple_of(position * length, length), length)
        result = sums[rows, :] + gain_ref[:, lanes] * conv_ref[rows, :]
        mixed_ref[:, lanes] = (result * silu(z_ref[:, lanes].astype(jnp.float32))).astype(jnp.bfloat16)
        return carry

    lax.fori_loop(0, tiles, out_tile, 0)

    @pl.when(me < count - 1)
    def _():
        rim_copy.wait_send()

    pass_on(me, True, True, sent)
    for hop in range(1, planes):
        column_step(hop, sent, False)
    for hop in range(planes):
        across_step(hop, sent, False)


def shards(
    inner_x,
    inner_z,
    step_raw,
    conv_weight,
    state_proj,
    step_bias,
    decay_log,
    skip_gain,
    moe_tokens,
    routes,
    gate_weight,
    up_weight,
):
    length, channels = inner_x.shape
    states = decay_log.shape[0]
    count, flight = lax.axis_size("seq"), lax.axis_size("exp")
    hidden_rows, features = gate_weight.shape[1:]
    width = moe_tokens.shape[1]
    tiles = channels // LANES
    piece = tiles * states // count
    spread = max(1, piece // states)
    slots = CAP * count
    whole, half = jnp.float32, jnp.bfloat16
    flat = pltpu.VMEM((tiles * length, LANES), whole)
    table = pltpu.VMEM((states * length, LANES), whole)
    held = pltpu.VMEM((tiles * states, LANES), whole)
    pieces = pltpu.VMEM((count, piece, LANES), half)
    totals = pltpu.VMEM((count, spread, LANES), whole)
    block = (16, width + width // 4)
    dma = pltpu.SemaphoreType.DMA
    in_vmem = pl.BlockSpec(memory_space=pltpu.VMEM)
    in_hbm = pl.BlockSpec(memory_space=pl.ANY)
    mixed, hidden = pl.pallas_call(
        functools.partial(mixer_kernel, count, flight),
        out_shape=(
            jax.ShapeDtypeStruct((length, channels), half),
            jax.ShapeDtypeStruct((hidden_rows, slots), half),
        ),
        in_specs=[in_vmem] * 10 + [in_hbm] * 2,
        out_specs=(in_vmem, in_vmem),
        scratch_shapes=[
            pltpu.VMEM((hidden_rows, features), half),
            pltpu.VMEM((hidden_rows, features), half),
            pltpu.VMEM((16, channels), half),
            pltpu.VMEM((length + 16, LANES), whole),
            pltpu.VMEM((length, channels), half),
            flat,
            flat,
            flat,
            pltpu.VMEM((flight, length, 2 * states), whole),
            pltpu.VMEM((length, 2 * states), whole),
            table,
            table,
            held,
            held,
            pltpu.VMEM((tiles, LANES), whole),
            pieces,
            totals,
            pieces,
            totals,
            pieces,
            pieces,
            held,
            flat,
            pltpu.VMEM((flight, *block), half),
            pltpu.VMEM((count, flight, *block), half),
            pltpu.VMEM((slots, features), half),
            pltpu.VMEM((slots, slots), half),
            dma((2,)),
            dma((2,)),
            dma((2, flight)),
            dma((2, flight)),
            dma((4, count)),
            dma((count,)),
            dma((3, count)),
            dma((3, count)),
        ],
        compiler_params=pltpu.CompilerParams(
            vmem_limit_bytes=VMEM_LIMIT, collective_id=0, has_side_effects=True
        ),
    )(
        inner_x, inner_z, step_raw, conv_weight, state_proj, step_bias[None, :], decay_log, skip_gain[None, :],
        moe_tokens, routes.T, gate_weight[0], up_weight[0],
    )
    return (mixed, hidden[None])


def solution(mesh):
    return jax.shard_map(
        shards,
        mesh=mesh,
        in_specs=(
            P("seq", "exp"),
            P("seq", "exp"),
            P("seq", "exp"),
            P(None, "exp"),
            P("exp", None),
            P("exp"),
            P(None, "exp"),
            P("exp"),
            P("seq", "exp"),
            P("seq", None),
            P("exp", "seq", None),
            P("exp", "seq", None),
        ),
        out_specs=(P("seq", "exp"), P("exp", "seq", None)),
        check_vma=False,
    )
```

```python
import functools

import jax
import jax.numpy as jnp
from jax import lax
from jax.experimental import pallas as pl
from jax.experimental.pallas import tpu as pltpu
from jax.sharding import PartitionSpec as P

CAP = 20
LANES = 128
SUB = 8
LOG2E = 1.4426950408889634
MESH = pl.DeviceIdType.MESH
VMEM_LIMIT = 60 * 1024 * 1024


def silu(value):
    half = 0.5 * value
    return half + half * jnp.tanh(half)


def softplus(value):
    grown = jnp.exp(value)
    series = grown * (1.0 - grown * (0.5 - grown * (1.0 / 3.0 - 0.25 * grown)))
    return jnp.where(grown < 0.03, series, jnp.log(1.0 + grown))


def splat_columns(coef_ref, first, count, table):
    length = coef_ref.shape[0]
    for column in range(count):
        table[pl.ds(column * length, length), :] = jnp.broadcast_to(
            coef_ref[:, first + column : first + column + 1], (length, LANES)
        )


def rate_rows(decay_ref, table):
    states, channels = decay_ref.shape

    def tile(position, carry):
        lanes = pl.ds(pl.multiple_of(position * LANES, LANES), LANES)
        rows = pl.ds(pl.multiple_of(position * states, states), states)
        table[rows, :] = jnp.exp(decay_ref[:, lanes]) * (-LOG2E)
        return carry

    lax.fori_loop(0, channels // LANES, tile, 0)


def mixer_kernel(
    count, flight, x_hbm, z_hbm, raw_hbm, taps_hbm, proj_hbm, bias_hbm, decay_hbm, gain_hbm, tokens_hbm, routes_hbm,
    gate_hbm, up_hbm, mixed_ref, hidden_ref,
    x_ref, z_ref, raw_ref, taps_ref, proj_ref, bias_ref, decay_ref, gain_ref, tokens_ref, routes_ref,
    gate_ref, up_ref, rim_ref, wide, rounded, conv_ref, step_ref, drive_ref, parts_ref, coef_ref, in_table, out_table,
    rate_ref, end_ref, total_ref, end_out, total_out, got_end, got_total, leaving, entering, start_ref, sums,
    stage, block_rows, rows_ref, order_ref,
    local_sem, rim_sem, pair_out, pair_in, rows_out, rows_in, sends, arrivals,
):
    length, channels = x_ref.shape
    states = decay_ref.shape[0]
    taps = taps_ref.shape[0]
    width = tokens_ref.shape[1]
    quarter = width // 4
    tiles = channels // LANES
    piece = tiles * states // count
    spread = got_total.shape[1]
    hidden_rows = gate_ref.shape[0]
    chunk = 256 if hidden_rows % 256 == 0 else hidden_rows
    me, side = lax.axis_index("seq"), lax.axis_index("exp")

    def seq_peer(distance):
        return lax.rem(me + distance, count)

    def exp_peer(distance):
        return lax.rem(side + distance, flight)

    loads = [
        pltpu.make_async_copy(source, target, local_sem.at[number])
        for number, (source, target) in enumerate(
            (
                (routes_hbm, routes_ref), (tokens_hbm, tokens_ref), (raw_hbm, raw_ref), (bias_hbm, bias_ref),
                (decay_hbm, decay_ref), (x_hbm, x_ref), (taps_hbm, taps_ref), (proj_hbm, proj_ref),
                (z_hbm, z_ref), (gain_hbm, gain_ref), (gate_hbm, gate_ref), (up_hbm, up_ref),
            )
        )
    ]
    for load in loads:
        load.start()

    barrier = pltpu.get_barrier_semaphore()

    def greet(distance, carry):
        pl.semaphore_signal(barrier, inc=1, device_id=(seq_peer(distance), side), device_id_type=MESH)
        return carry

    lax.fori_loop(1, count, greet, 0)
    for distance in range(1, flight):
        pl.semaphore_signal(barrier, inc=1, device_id=(me, exp_peer(distance)), device_id_type=MESH)
    pl.semaphore_wait(barrier, count - 1 + flight - 1)

    def remote(source, target, send_sem, arrive_sem, seq_index, exp_index):
        return pltpu.make_async_remote_copy(
            source, target, send_sem, arrive_sem, device_id=(seq_index, exp_index), device_id_type=MESH
        )

    rim_copy = remote(
        x_hbm.at[pl.ds(length - 16, 16), :], rim_ref, rim_sem.at[0], rim_sem.at[1], seq_peer(1), side
    )

    @pl.when(me < count - 1)
    def _():
        rim_copy.start()

    above = lax.broadcasted_iota(jnp.int32, (length, length), 0) < lax.broadcasted_iota(
        jnp.int32, (length, length), 1
    )
    above = above.astype(jnp.float32).astype(jnp.bfloat16)
    slot = lax.broadcasted_iota(jnp.int32, (16, length), 0)
    for load in loads[:2]:
        load.wait()
    for expert in range(flight):
        named = (routes_ref[pl.ds(0, 1), :] == expert).astype(jnp.float32)
        for choice in range(1, routes_ref.shape[0]):
            named = named + (routes_ref[pl.ds(choice, 1), :] == expert).astype(jnp.float32)
        named = jnp.broadcast_to(named, (16, length))
        rank = jnp.dot(named.astype(jnp.bfloat16), above, preferred_element_type=jnp.float32)
        taken = jnp.where(rank == slot.astype(jnp.float32), named, 0.0).astype(jnp.bfloat16)
        stage[expert, :, pl.ds(0, width)] = jnp.dot(
            taken, tokens_ref[...], preferred_element_type=jnp.float32
        ).astype(jnp.bfloat16)
        late = jnp.where(rank == (16 + (slot & 3)).astype(jnp.float32), named, 0.0)
        rest = jnp.zeros((16, quarter), jnp.float32)
        for part in range(4):
            mine = jnp.where((slot >> 2) == part, late, 0.0).astype(jnp.bfloat16)
            rest = rest + jnp.dot(
                mine, tokens_ref[:, pl.ds(part * quarter, quarter)], preferred_element_type=jnp.float32
            )
        stage[expert, :, pl.ds(width, quarter)] = rest.astype(jnp.bfloat16)

    def stage_copy(distance):
        return remote(
            stage.at[exp_peer(distance)], block_rows.at[me, side],
            pair_out.at[0, distance], pair_in.at[0, distance], me, exp_peer(distance),
        )

    def coef_copy(distance):
        return remote(
            parts_ref.at[side], parts_ref.at[side],
            pair_out.at[1, distance], pair_in.at[1, distance], me, exp_peer(distance),
        )

    for distance in range(1, flight):
        stage_copy(distance).start()
    block_rows[me, side] = stage[side]

    def step_tile(position, carry):
        lanes = pl.ds(pl.multiple_of(position * LANES, LANES), LANES)
        rows = pl.ds(pl.multiple_of(position * length, length), length)
        step_ref[rows, :] = softplus(raw_ref[:, lanes].astype(jnp.float32) + bias_ref[:, lanes])
        return carry

    for load in loads[2:4]:
        load.wait()
    lax.fori_loop(0, tiles // 2, step_tile, 0)

    low = lax.rem(me, 4)
    plane = me // 4
    planes = count // 4
    across = me - low + lax.rem(low + 2, 4)
    beside = me + 1 - 2 * lax.rem(me, 2)
    far = across + 1 - 2 * lax.rem(across, 2)

    def row_copy(kind, source):
        target = (me + 4, me - 4, across, beside)[kind]
        return remote(
            block_rows.at[source], block_rows.at[source], rows_out.at[kind, source], rows_in.at[source], target, side
        )

    def arrived(source):
        row_copy(3, source).wait_recv()

    def pass_on(source, up, down, act):
        if up:
            pl.when(plane < planes - 1)(lambda: act(row_copy(0, source)))
        if down:
            pl.when(plane > 0)(lambda: act(row_copy(1, source)))
        act(row_copy(2, source))
        act(row_copy(3, source))

    def column_step(hop, act, wait):
        @pl.when(plane >= hop)
        def _():
            if wait:
                arrived(me - 4 * hop)
            pass_on(me - 4 * hop, True, False, act)

        @pl.when(plane + hop < planes)
        def _():
            if wait:
                arrived(me + 4 * hop)
            pass_on(me + 4 * hop, False, True, act)

    def across_step(hop, act, wait):
        if hop == 0:
            if wait:
                arrived(across)
            act(row_copy(3, across))
            return

        @pl.when(plane >= hop)
        def _():
            if wait:
                arrived(across - 4 * hop)
            act(row_copy(3, across - 4 * hop))

        @pl.when(plane + hop < planes)
        def _():
            if wait:
                arrived(across + 4 * hop)
            act(row_copy(3, across + 4 * hop))

    def start(copy):
        copy.start()

    def sent(copy):
        copy.wait_send()

    for distance in range(1, flight):
        stage_copy(distance).wait()
    pass_on(me, True, True, start)
    lax.fori_loop(tiles // 2, tiles, step_tile, 0)
    loads[4].wait()
    rate_rows(decay_ref, rate_ref)
    held_at = lax.broadcasted_iota(jnp.int32, order_ref.shape, 1)
    wanted = lax.broadcasted_iota(jnp.int32, order_ref.shape, 0)
    tail_at = held_at - 16 * count
    goes_to = jnp.where(
        held_at < 16 * count,
        (held_at >> 4) * CAP + (held_at & 15),
        (tail_at >> 2) * CAP + 16 + (tail_at & 3),
    )
    order_ref[...] = (goes_to == wanted).astype(jnp.float32).astype(jnp.bfloat16)
    for load in loads[5:8]:
        load.wait()

    @pl.when(me > 0)
    def _():
        rim_copy.wait_recv()

    @pl.when(me == 0)
    def _():
        rim_ref[...] = jnp.zeros_like(rim_ref)

    def conv_tile(position, carry):
        lanes = pl.ds(pl.multiple_of(position * LANES, LANES), LANES)
        rows = pl.ds(pl.multiple_of(position * length, length), length)
        wide[pl.ds(0, 16), :] = rim_ref[:, lanes].astype(jnp.float32)
        wide[pl.ds(16, length), :] = x_ref[:, lanes].astype(jnp.float32)
        total = taps_ref[pl.ds(0, 1), lanes] * wide[pl.ds(17 - taps, length), :]
        for tap in range(1, taps):
            total = total + taps_ref[pl.ds(tap, 1), lanes] * wide[pl.ds(17 - taps + tap, length), :]
        conv = silu(total)
        conv_ref[rows, :] = conv
        drive_ref[rows, :] = step_ref[rows, :] * conv
        rounded[:, lanes] = conv.astype(jnp.bfloat16)
        return carry

    lax.fori_loop(0, tiles // 2, conv_tile, 0)
    if planes > 1:
        column_step(1, start, True)
    lax.fori_loop(tiles // 2, tiles, conv_tile, 0)
    dims = (((1,), (1,)), ((), ()))
    parts_ref[side] = lax.dot_general(rounded[...], proj_ref[...], dims, preferred_element_type=jnp.float32)
    for distance in range(1, flight):
        coef_copy(distance).start()
    if planes > 2:
        column_step(2, start, True)
    for distance in range(1, flight):
        coef_copy(distance).wait()
    coef = parts_ref[0]
    for other in range(1, flight):
        coef = coef + parts_ref[other]
    coef_ref[...] = coef
    splat_columns(coef_ref, 0, states, in_table)
    splat_columns(coef_ref, states, states, out_table)

    groups = tiles // SUB
    pair = 2 if groups % 2 == 0 else 1
    span = states // pair

    def lines(ref, group, offset, stride):
        return ref[pl.ds(group * SUB * stride + offset, SUB, stride=stride), :]

    def sweep(first, lead, begin, output):
        rates = [[lines(rate_ref, first + g, lead + n, states) for n in range(span)] for g in range(pair)]
        keep_total = lead == 0 and not output

        def block(turn, held):
            state = [list(held[g * span : (g + 1) * span]) for g in range(pair)]
            totals = list(held[pair * span :])
            for inner in range(4):
                t = turn * 4 + inner
                steps = [lines(step_ref, first + g, t, length) for g in range(pair)]
                drives = [lines(drive_ref, first + g, t, length) for g in range(pair)]
                if keep_total:
                    totals = [totals[g] + steps[g] for g in range(pair)]
                terms = [[None, None] for _ in range(pair)]
                for n in range(span):
                    row = in_table[pl.ds((lead + n) * length + t, 1), :]
                    if output:
                        out_row = out_table[pl.ds((lead + n) * length + t, 1), :]
                    for g in range(pair):
                        state[g][n] = jnp.exp2(rates[g][n] * steps[g]) * state[g][n] + row * drives[g]
                        if output:
                            term = out_row * state[g][n]
                            old = terms[g][n % 2]
                            terms[g][n % 2] = term if old is None else old + term
                if output:
                    for g in range(pair):
                        where = pl.ds((first + g) * SUB * length + t, SUB, stride=length)
                        part = terms[g][0] if span == 1 else terms[g][0] + terms[g][1]
                        sums[where, :] = part if lead == 0 else sums[where, :] + part
            return tuple(s for line in state for s in line) + tuple(totals)

        zeros = (jnp.zeros((SUB, LANES), jnp.float32),) * (pair if keep_total else 0)
        held = lax.fori_loop(0, length // 4, block, tuple(begin) + zeros)
        if keep_total:
            for g in range(pair):
                total_ref[pl.ds(pl.multiple_of((first + g) * SUB, SUB), SUB), :] = held[pair * span + g]
        return held

    def carry_copy(kind, distance):
        peer = seq_peer(distance)
        source = (end_out.at[peer], total_out.at[peer], leaving.at[peer])[kind]
        target = (got_end.at[me], got_total.at[me], entering.at[me])[kind]
        return remote(source, target, sends.at[kind, distance], arrivals.at[kind, distance], peer, side)

    def send_ends(begin, stop):
        def one(peer, carry):
            end_out[peer] = end_ref[pl.ds(peer * piece, piece), :].astype(jnp.bfloat16)
            total_out[peer] = total_ref[pl.ds(peer * piece // states, spread), :]

            @pl.when(peer != me)
            def _():
                distance = lax.rem(peer - me + count, count)
                carry_copy(0, distance).start()
                carry_copy(1, distance).start()

            return carry

        lax.fori_loop(begin, stop, one, 0)

    events = [lambda hop=hop: column_step(hop, start, True) for hop in range(3, planes)]
    events += [lambda hop=hop: across_step(hop, start, True) for hop in range(planes)]
    units = [(first, lead) for first in range(0, groups, pair) for lead in range(0, states, span)]
    for number, (first, lead) in enumerate(units):
        zero = jnp.zeros((SUB, LANES), jnp.float32)
        held = sweep(first, lead, (zero,) * (pair * span), False)
        for g in range(pair):
            for n in range(span):
                end_ref[pl.ds((first + g) * SUB * states + lead + n, SUB, stride=states), :] = held[g * span + n]
        if lead + span == states:
            send_ends(count * first // groups, count * (first + pair) // groups)
        for _ in range(0 if number == len(units) - 1 else min(len(events), 1 + (number == 0))):
            events.pop(0)()
    got_end[me] = end_out[me]
    got_total[me] = total_out[me]
    for event in events:
        event()

    def last_rows(turn, carry):
        arrived(lax.rem(beside, 4) + 4 * turn)
        arrived(lax.rem(far, 4) + 4 * turn)
        return carry

    lax.fori_loop(0, planes, last_rows, 0)

    small = 4 * count
    for half in range(flight):
        def lay_rows(source, carry):
            rows_ref[pl.ds(pl.multiple_of(source * 16, 16), 16), pl.ds(half * width, width)] = block_rows[
                source, half, :, pl.ds(0, width)
            ]
            return carry

        lax.fori_loop(0, count, lay_rows, 0)
        rest = block_rows[:, half, :, pl.ds(width, quarter)].reshape(16 * count, quarter)
        into = lax.broadcasted_iota(jnp.int32, (small, 16 * count), 0)
        out_of = lax.broadcasted_iota(jnp.int32, (small, 16 * count), 1)
        for part in range(4):
            pick = ((into >> 2) * 16 + part * 4 + (into & 3) == out_of).astype(jnp.float32).astype(jnp.bfloat16)
            rows_ref[pl.ds(16 * count, small), pl.ds(half * width + part * quarter, quarter)] = jnp.dot(
                pick, rest, preferred_element_type=jnp.float32
            ).astype(jnp.bfloat16)
    def receive(distance, carry):
        carry_copy(0, distance).wait()
        carry_copy(1, distance).wait()
        return carry

    lax.fori_loop(1, count, receive, 0)
    own_rates = rate_ref[pl.ds(me * piece, piece), :]

    def join(source, state):
        leaving[source] = state.astype(jnp.bfloat16)
        totals = got_total[source]
        totals = jnp.broadcast_to(totals[:, None, :], (spread, piece // spread, LANES)).reshape(piece, LANES)
        return jnp.exp2(own_rates * totals) * state + got_end[source].astype(jnp.float32)

    lax.fori_loop(0, count, join, jnp.zeros((piece, LANES), jnp.float32), unroll=4)

    def send_back(distance, carry):
        carry_copy(2, distance).start()
        return carry

    lax.fori_loop(1, count, send_back, 0)
    entering[me] = leaving[me]
    for load in loads[8:]:
        load.wait()
    for turn in range(hidden_rows // chunk):
        part = pl.ds(turn * chunk, chunk)
        gate = lax.dot_general(rows_ref[...], gate_ref[part, :], dims, preferred_element_type=jnp.float32)
        up = lax.dot_general(rows_ref[...], up_ref[part, :], dims, preferred_element_type=jnp.float32)
        value = (silu(gate) * up).astype(jnp.bfloat16)
        hidden_ref[:, part] = jnp.dot(order_ref[...], value, preferred_element_type=jnp.float32).astype(
            jnp.bfloat16
        )

    def receive_back(distance, carry):
        carry_copy(2, distance).wait()
        return carry

    lax.fori_loop(1, count, receive_back, 0)

    def widen(source, carry):
        start_ref[pl.ds(source * piece, piece), :] = entering[source].astype(jnp.float32)
        return carry

    lax.fori_loop(0, count, widen, 0)

    def second(turn, carry):
        first = turn * pair
        for lead in range(0, states, span):
            begin = [lines(start_ref, first + g, lead + n, states) for g in range(pair) for n in range(span)]
            sweep(first, lead, begin, True)
        return carry

    lax.fori_loop(0, groups // pair, second, 0)

    def out_tile(position, carry):
        lanes = pl.ds(pl.multiple_of(position * LANES, LANES), LANES)
        rows = pl.ds(pl.multiple_of(position * length, length), length)
        result = sums[rows, :] + gain_ref[:, lanes] * conv_ref[rows, :]
        mixed_ref[:, lanes] = (result * silu(z_ref[:, lanes].astype(jnp.float32))).astype(jnp.bfloat16)
        return carry

    lax.fori_loop(0, tiles, out_tile, 0)

    @pl.when(me < count - 1)
    def _():
        rim_copy.wait_send()

    pass_on(me, True, True, sent)
    for hop in range(1, planes):
        column_step(hop, sent, False)
    for hop in range(planes):
        across_step(hop, sent, False)


def shards(
    inner_x,
    inner_z,
    step_raw,
    conv_weight,
    state_proj,
    step_bias,
    decay_log,
    skip_gain,
    moe_tokens,
    routes,
    gate_weight,
    up_weight,
):
    length, channels = inner_x.shape
    states = decay_log.shape[0]
    count, flight = lax.axis_size("seq"), lax.axis_size("exp")
    hidden_rows, features = gate_weight.shape[1:]
    width = moe_tokens.shape[1]
    tiles = channels // LANES
    piece = tiles * states // count
    spread = max(1, piece // states)
    slots = CAP * count
    whole, half = jnp.float32, jnp.bfloat16
    flat = pltpu.VMEM((tiles * length, LANES), whole)
    table = pltpu.VMEM((states * length, LANES), whole)
    held = pltpu.VMEM((tiles * states, LANES), whole)
    pieces = pltpu.VMEM((count, piece, LANES), half)
    totals = pltpu.VMEM((count, spread, LANES), whole)
    block = (16, width + width // 4)
    dma = pltpu.SemaphoreType.DMA
    in_vmem = pl.BlockSpec(memory_space=pltpu.VMEM)
    in_hbm = pl.BlockSpec(memory_space=pltpu.HBM)
    operands = (
        inner_x, inner_z, step_raw, conv_weight, state_proj.T, step_bias[None, :], decay_log, skip_gain[None, :],
        moe_tokens, routes.T,
    )
    mixed, hidden = pl.pallas_call(
        functools.partial(mixer_kernel, count, flight),
        out_shape=(
            jax.ShapeDtypeStruct((length, channels), half),
            jax.ShapeDtypeStruct((slots, hidden_rows), half),
        ),
        in_specs=[in_hbm] * 12,
        out_specs=(in_vmem, in_vmem),
        scratch_shapes=[
            *(pltpu.VMEM(operand.shape, operand.dtype) for operand in operands),
            pltpu.VMEM((hidden_rows, features), half),
            pltpu.VMEM((hidden_rows, features), half),
            pltpu.VMEM((16, channels), half),
            pltpu.VMEM((length + 16, LANES), whole),
            pltpu.VMEM((length, channels), half),
            flat,
            flat,
            flat,
            pltpu.VMEM((flight, length, 2 * states), whole),
            pltpu.VMEM((length, 2 * states), whole),
            table,
            table,
            held,
            held,
            pltpu.VMEM((tiles, LANES), whole),
            pieces,
            totals,
            pieces,
            totals,
            pieces,
            pieces,
            held,
            flat,
            pltpu.VMEM((flight, *block), half),
            pltpu.VMEM((count, flight, *block), half),
            pltpu.VMEM((slots, features), half),
            pltpu.VMEM((slots, slots), half),
            dma((12,)),
            dma((2,)),
            dma((2, flight)),
            dma((2, flight)),
            dma((4, count)),
            dma((count,)),
            dma((3, count)),
            dma((3, count)),
        ],
        compiler_params=pltpu.CompilerParams(
            vmem_limit_bytes=VMEM_LIMIT, collective_id=0, has_side_effects=True
        ),
    )(*operands, gate_weight[0], up_weight[0])
    return (mixed, hidden.T[None])


def solution(mesh):
    return jax.shard_map(
        shards,
        mesh=mesh,
        in_specs=(
            P("seq", "exp"),
            P("seq", "exp"),
            P("seq", "exp"),
            P(None, "exp"),
            P("exp", None),
            P("exp"),
            P(None, "exp"),
            P("exp"),
            P("seq", "exp"),
            P("seq", None),
            P("exp", "seq", None),
            P("exp", "seq", None),
        ),
        out_specs=(P("seq", "exp"), P("exp", "seq", None)),
        check_vma=False,
    )
```

```python
import functools

import jax
import jax.numpy as jnp
from jax import lax
from jax.experimental import pallas as pl
from jax.experimental.pallas import tpu as pltpu
from jax.sharding import PartitionSpec as P

CAP = 20
TURN = 8
LANES = 128
SUB = 8
LOG2E = 1.4426950408889634
MESH = pl.DeviceIdType.MESH
VMEM_LIMIT = 60 * 1024 * 1024


def silu(value):
    half = 0.5 * value
    return half + half * jnp.tanh(half)


def softplus(value):
    grown = jnp.exp(value)
    series = grown * (1.0 - grown * (0.5 - grown * (1.0 / 3.0 - 0.25 * grown)))
    return jnp.where(grown < 0.03, series, jnp.log(1.0 + grown))


def splat_columns(coef_ref, first, count, table):
    length = coef_ref.shape[0]
    for column in range(count):
        table[pl.ds(column * length, length), :] = jnp.broadcast_to(
            coef_ref[:, first + column : first + column + 1], (length, LANES)
        )


def rate_rows(decay_ref, table):
    states, channels = decay_ref.shape

    def tile(position, carry):
        lanes = pl.ds(pl.multiple_of(position * LANES, LANES), LANES)
        rows = pl.ds(pl.multiple_of(position * states, states), states)
        table[rows, :] = jnp.exp(decay_ref[:, lanes]) * (-LOG2E)
        return carry

    lax.fori_loop(0, channels // LANES, tile, 0)


def mixer_kernel(
    count, flight, x_hbm, z_hbm, raw_hbm, taps_hbm, proj_hbm, bias_hbm, decay_hbm, gain_hbm, tokens_hbm, routes_hbm,
    gate_hbm, up_hbm, mixed_ref, hidden_ref,
    x_ref, z_ref, raw_ref, taps_ref, proj_ref, bias_ref, decay_ref, gain_ref, tokens_ref, routes_ref,
    gate_ref, up_ref, rim_ref, wide, rounded, conv_ref, step_ref, drive_ref, parts_ref, coef_ref, in_table, out_table,
    rate_ref, end_ref, total_ref, end_out, got_end, leaving, entering, start_ref, sums,
    stage, block_rows, rows_ref, order_ref,
    local_sem, rim_sem, pair_out, pair_in, rows_out, rows_in, sends, arrivals,
):
    length, channels = x_ref.shape
    states = decay_ref.shape[0]
    taps = taps_ref.shape[0]
    width = tokens_ref.shape[1]
    quarter = width // 4
    tiles = channels // LANES
    piece = tiles * states // count
    spread = max(1, piece // states)
    lead_rows = -(-piece // 16) * 16
    extra_rows = end_out.shape[1] - lead_rows
    hidden_rows = gate_ref.shape[0]
    chunk = 256 if hidden_rows % 256 == 0 else hidden_rows
    me, side = lax.axis_index("seq"), lax.axis_index("exp")

    def seq_peer(distance):
        return lax.rem(me + distance, count)

    def exp_peer(distance):
        return lax.rem(side + distance, flight)

    loads = [
        pltpu.make_async_copy(source, target, local_sem.at[number])
        for number, (source, target) in enumerate(
            (
                (routes_hbm, routes_ref), (tokens_hbm, tokens_ref), (raw_hbm, raw_ref), (bias_hbm, bias_ref),
                (decay_hbm, decay_ref), (x_hbm, x_ref), (taps_hbm, taps_ref), (proj_hbm, proj_ref),
                (z_hbm, z_ref), (gain_hbm, gain_ref), (gate_hbm, gate_ref), (up_hbm, up_ref),
            )
        )
    ]
    for load in loads:
        load.start()

    barrier = pltpu.get_barrier_semaphore()

    def greet(distance, carry):
        pl.semaphore_signal(barrier, inc=1, device_id=(seq_peer(distance), side), device_id_type=MESH)
        return carry

    lax.fori_loop(1, count, greet, 0)
    for distance in range(1, flight):
        pl.semaphore_signal(barrier, inc=1, device_id=(me, exp_peer(distance)), device_id_type=MESH)
    pl.semaphore_wait(barrier, count - 1 + flight - 1)

    def remote(source, target, send_sem, arrive_sem, seq_index, exp_index):
        return pltpu.make_async_remote_copy(
            source, target, send_sem, arrive_sem, device_id=(seq_index, exp_index), device_id_type=MESH
        )

    rim_copy = remote(
        x_hbm.at[pl.ds(length - 16, 16), :], rim_ref, rim_sem.at[0], rim_sem.at[1], seq_peer(1), side
    )

    @pl.when(me < count - 1)
    def _():
        rim_copy.start()

    above = lax.broadcasted_iota(jnp.int32, (length, length), 0) < lax.broadcasted_iota(
        jnp.int32, (length, length), 1
    )
    above = above.astype(jnp.float32).astype(jnp.bfloat16)
    slot = lax.broadcasted_iota(jnp.int32, (16, length), 0)
    for load in loads[:2]:
        load.wait()
    for expert in range(flight):
        named = (routes_ref[pl.ds(0, 1), :] == expert).astype(jnp.float32)
        for choice in range(1, routes_ref.shape[0]):
            named = named + (routes_ref[pl.ds(choice, 1), :] == expert).astype(jnp.float32)
        named = jnp.broadcast_to(named, (16, length))
        rank = jnp.dot(named.astype(jnp.bfloat16), above, preferred_element_type=jnp.float32)
        taken = jnp.where(rank == slot.astype(jnp.float32), named, 0.0).astype(jnp.bfloat16)
        stage[expert, :, pl.ds(0, width)] = jnp.dot(
            taken, tokens_ref[...], preferred_element_type=jnp.float32
        ).astype(jnp.bfloat16)
        late = jnp.where(rank == (16 + (slot & 3)).astype(jnp.float32), named, 0.0)
        rest = jnp.zeros((16, quarter), jnp.float32)
        for part in range(4):
            mine = jnp.where((slot >> 2) == part, late, 0.0).astype(jnp.bfloat16)
            rest = rest + jnp.dot(
                mine, tokens_ref[:, pl.ds(part * quarter, quarter)], preferred_element_type=jnp.float32
            )
        stage[expert, :, pl.ds(width, quarter)] = rest.astype(jnp.bfloat16)

    def stage_copy(distance):
        return remote(
            stage.at[exp_peer(distance)], block_rows.at[me, side],
            pair_out.at[0, distance], pair_in.at[0, distance], me, exp_peer(distance),
        )

    def coef_copy(distance):
        return remote(
            parts_ref.at[side], parts_ref.at[side],
            pair_out.at[1, distance], pair_in.at[1, distance], me, exp_peer(distance),
        )

    for distance in range(1, flight):
        stage_copy(distance).start()
    block_rows[me, side] = stage[side]

    def step_tile(position, carry):
        lanes = pl.ds(pl.multiple_of(position * LANES, LANES), LANES)
        rows = pl.ds(pl.multiple_of(position * length, length), length)
        step_ref[rows, :] = softplus(raw_ref[:, lanes].astype(jnp.float32) + bias_ref[:, lanes])
        return carry

    for load in loads[2:4]:
        load.wait()
    lax.fori_loop(0, tiles // 2, step_tile, 0)

    low = lax.rem(me, 4)
    plane = me // 4
    planes = count // 4
    across = me - low + lax.rem(low + 2, 4)
    beside = me + 1 - 2 * lax.rem(me, 2)
    far = across + 1 - 2 * lax.rem(across, 2)

    def row_copy(kind, source):
        target = (me + 4, me - 4, across, beside)[kind]
        return remote(
            block_rows.at[source], block_rows.at[source], rows_out.at[kind, source], rows_in.at[source], target, side
        )

    def arrived(source):
        row_copy(3, source).wait_recv()

    def pass_on(source, up, down, act):
        if up:
            pl.when(plane < planes - 1)(lambda: act(row_copy(0, source)))
        if down:
            pl.when(plane > 0)(lambda: act(row_copy(1, source)))
        act(row_copy(2, source))
        act(row_copy(3, source))

    def column_step(hop, act, wait):
        @pl.when(plane >= hop)
        def _():
            if wait:
                arrived(me - 4 * hop)
            pass_on(me - 4 * hop, True, False, act)

        @pl.when(plane + hop < planes)
        def _():
            if wait:
                arrived(me + 4 * hop)
            pass_on(me + 4 * hop, False, True, act)

    def across_step(hop, act, wait):
        if hop == 0:
            if wait:
                arrived(across)
            act(row_copy(3, across))
            return

        @pl.when(plane >= hop)
        def _():
            if wait:
                arrived(across - 4 * hop)
            act(row_copy(3, across - 4 * hop))

        @pl.when(plane + hop < planes)
        def _():
            if wait:
                arrived(across + 4 * hop)
            act(row_copy(3, across + 4 * hop))

    def start(copy):
        copy.start()

    def sent(copy):
        copy.wait_send()

    for distance in range(1, flight):
        stage_copy(distance).wait()
    pass_on(me, True, True, start)
    lax.fori_loop(tiles // 2, tiles, step_tile, 0)
    loads[4].wait()
    rate_rows(decay_ref, rate_ref)
    held_at = lax.broadcasted_iota(jnp.int32, order_ref.shape, 1)
    wanted = lax.broadcasted_iota(jnp.int32, order_ref.shape, 0)
    tail_at = held_at - 16 * count
    goes_to = jnp.where(
        held_at < 16 * count,
        (held_at >> 4) * CAP + (held_at & 15),
        (tail_at >> 2) * CAP + 16 + (tail_at & 3),
    )
    order_ref[...] = (goes_to == wanted).astype(jnp.float32).astype(jnp.bfloat16)
    for load in loads[5:8]:
        load.wait()

    @pl.when(me > 0)
    def _():
        rim_copy.wait_recv()

    @pl.when(me == 0)
    def _():
        rim_ref[...] = jnp.zeros_like(rim_ref)

    def conv_tile(position, carry):
        lanes = pl.ds(pl.multiple_of(position * LANES, LANES), LANES)
        rows = pl.ds(pl.multiple_of(position * length, length), length)
        wide[pl.ds(0, 16), :] = rim_ref[:, lanes].astype(jnp.float32)
        wide[pl.ds(16, length), :] = x_ref[:, lanes].astype(jnp.float32)
        total = taps_ref[pl.ds(0, 1), lanes] * wide[pl.ds(17 - taps, length), :]
        for tap in range(1, taps):
            total = total + taps_ref[pl.ds(tap, 1), lanes] * wide[pl.ds(17 - taps + tap, length), :]
        conv = silu(total)
        conv_ref[rows, :] = conv
        drive_ref[rows, :] = step_ref[rows, :] * conv
        rounded[:, lanes] = conv.astype(jnp.bfloat16)
        return carry

    lax.fori_loop(0, tiles // 2, conv_tile, 0)
    if planes > 1:
        column_step(1, start, True)
    lax.fori_loop(tiles // 2, tiles, conv_tile, 0)
    dims = (((1,), (1,)), ((), ()))
    parts_ref[side] = lax.dot_general(rounded[...], proj_ref[...], dims, preferred_element_type=jnp.float32)
    for distance in range(1, flight):
        coef_copy(distance).start()
    if planes > 2:
        column_step(2, start, True)
    for distance in range(1, flight):
        coef_copy(distance).wait()
    coef = parts_ref[0]
    for other in range(1, flight):
        coef = coef + parts_ref[other]
    coef_ref[...] = coef
    splat_columns(coef_ref, 0, states, in_table)
    splat_columns(coef_ref, states, states, out_table)

    groups = tiles // SUB
    pair = 2 if groups % 2 == 0 else 1
    span = states // pair

    def lines(ref, group, offset, stride):
        return ref[pl.ds(group * SUB * stride + offset, SUB, stride=stride), :]

    def sweep(first, lead, begin, output):
        rates = [[lines(rate_ref, first + g, lead + n, states) for n in range(span)] for g in range(pair)]
        keep_total = lead == 0 and not output

        def block(turn, held):
            state = [list(held[g * span : (g + 1) * span]) for g in range(pair)]
            totals = list(held[pair * span :])
            for inner in range(TURN):
                t = turn * TURN + inner
                steps = [lines(step_ref, first + g, t, length) for g in range(pair)]
                drives = [lines(drive_ref, first + g, t, length) for g in range(pair)]
                if keep_total:
                    totals = [totals[g] + steps[g] for g in range(pair)]
                terms = [[None, None] for _ in range(pair)]
                for n in range(span):
                    row = in_table[pl.ds((lead + n) * length + t, 1), :]
                    if output:
                        out_row = out_table[pl.ds((lead + n) * length + t, 1), :]
                    for g in range(pair):
                        state[g][n] = jnp.exp2(rates[g][n] * steps[g]) * state[g][n] + row * drives[g]
                        if output:
                            term = out_row * state[g][n]
                            old = terms[g][n % 2]
                            terms[g][n % 2] = term if old is None else old + term
                if output:
                    for g in range(pair):
                        where = pl.ds((first + g) * SUB * length + t, SUB, stride=length)
                        part = terms[g][0] if span == 1 else terms[g][0] + terms[g][1]
                        sums[where, :] = part if lead == 0 else sums[where, :] + part
            return tuple(s for line in state for s in line) + tuple(totals)

        zeros = (jnp.zeros((SUB, LANES), jnp.float32),) * (pair if keep_total else 0)
        held = lax.fori_loop(0, length // TURN, block, tuple(begin) + zeros)
        if keep_total:
            for g in range(pair):
                total_ref[pl.ds(pl.multiple_of((first + g) * SUB, SUB), SUB), :] = held[pair * span + g]
        return held

    def carry_copy(kind, distance):
        peer = seq_peer(distance)
        source = (end_out.at[peer], leaving.at[peer])[kind]
        target = (got_end.at[me], entering.at[me])[kind]
        return remote(source, target, sends.at[kind, distance], arrivals.at[kind, distance], peer, side)

    def send_ends(begin, stop):
        def one(peer, carry):
            end_out[peer, pl.ds(0, piece), :] = end_ref[pl.ds(peer * piece, piece), :].astype(jnp.bfloat16)
            line = lax.broadcasted_iota(jnp.int32, (extra_rows, LANES), 0)
            rest = jnp.zeros((extra_rows, LANES), jnp.float32)
            for row in range(spread):
                total = total_ref[pl.ds(peer * piece // states + row, 1), :]
                for part in range(3):
                    top = total.astype(jnp.bfloat16).astype(jnp.float32)
                    rest = jnp.where(line == part * spread + row, top, rest)
                    total = total - top
            end_out[peer, pl.ds(lead_rows, extra_rows), :] = rest.astype(jnp.bfloat16)

            @pl.when(peer != me)
            def _():
                distance = lax.rem(peer - me + count, count)
                carry_copy(0, distance).start()

            return carry

        lax.fori_loop(begin, stop, one, 0)

    events = [lambda hop=hop: column_step(hop, start, True) for hop in range(3, planes)]
    events += [lambda hop=hop: across_step(hop, start, True) for hop in range(planes)]
    units = [(first, lead) for first in range(0, groups, pair) for lead in range(0, states, span)]
    for number, (first, lead) in enumerate(units):
        zero = jnp.zeros((SUB, LANES), jnp.float32)
        held = sweep(first, lead, (zero,) * (pair * span), False)
        for g in range(pair):
            for n in range(span):
                end_ref[pl.ds((first + g) * SUB * states + lead + n, SUB, stride=states), :] = held[g * span + n]
        if lead + span == states:
            send_ends(count * first // groups, count * (first + pair) // groups)
        for _ in range(0 if number == len(units) - 1 else min(len(events), 1 + (number == 0))):
            events.pop(0)()
    got_end[me] = end_out[me]
    for event in events:
        event()

    def last_rows(turn, carry):
        arrived(lax.rem(beside, 4) + 4 * turn)
        arrived(lax.rem(far, 4) + 4 * turn)
        return carry

    lax.fori_loop(0, planes, last_rows, 0)

    small = 4 * count
    for half in range(flight):
        def lay_rows(source, carry):
            rows_ref[pl.ds(pl.multiple_of(source * 16, 16), 16), pl.ds(half * width, width)] = block_rows[
                source, half, :, pl.ds(0, width)
            ]
            return carry

        lax.fori_loop(0, count, lay_rows, 0)
        rest = block_rows[:, half, :, pl.ds(width, quarter)].reshape(16 * count, quarter)
        into = lax.broadcasted_iota(jnp.int32, (small, 16 * count), 0)
        out_of = lax.broadcasted_iota(jnp.int32, (small, 16 * count), 1)
        for part in range(4):
            pick = ((into >> 2) * 16 + part * 4 + (into & 3) == out_of).astype(jnp.float32).astype(jnp.bfloat16)
            rows_ref[pl.ds(16 * count, small), pl.ds(half * width + part * quarter, quarter)] = jnp.dot(
                pick, rest, preferred_element_type=jnp.float32
            ).astype(jnp.bfloat16)
    def receive(distance, carry):
        carry_copy(0, distance).wait()
        return carry

    lax.fori_loop(1, count, receive, 0)
    own_rates = rate_ref[pl.ds(me * piece, piece), :]

    column = lax.broadcasted_iota(jnp.int32, (piece, extra_rows), 1)
    kept = lax.broadcasted_iota(jnp.int32, (piece, extra_rows), 0) // (piece // spread)
    adds = jnp.zeros((piece, extra_rows), jnp.float32)
    for part in range(3):
        adds = adds + (column == part * spread + kept).astype(jnp.float32)
    adds = adds.astype(jnp.bfloat16)

    def join(source, state):
        leaving[source] = state.astype(jnp.bfloat16)

        @pl.when(source != me)
        def _():
            carry_copy(1, lax.rem(source - me + count, count)).start()

        totals = jnp.dot(
            adds, got_end[source, pl.ds(lead_rows, extra_rows), :], preferred_element_type=jnp.float32
        )
        return jnp.exp2(own_rates * totals) * state + got_end[source, pl.ds(0, piece), :].astype(jnp.float32)

    lax.fori_loop(0, count, join, jnp.zeros((piece, LANES), jnp.float32), unroll=4)
    entering[me] = leaving[me]
    for load in loads[8:]:
        load.wait()
    for turn in range(hidden_rows // chunk):
        part = pl.ds(turn * chunk, chunk)
        gate = lax.dot_general(rows_ref[...], gate_ref[part, :], dims, preferred_element_type=jnp.float32)
        up = lax.dot_general(rows_ref[...], up_ref[part, :], dims, preferred_element_type=jnp.float32)
        value = (silu(gate) * up).astype(jnp.bfloat16)
        hidden_ref[:, part] = jnp.dot(order_ref[...], value, preferred_element_type=jnp.float32).astype(
            jnp.bfloat16
        )

    def receive_back(distance, carry):
        carry_copy(1, distance).wait()
        return carry

    lax.fori_loop(1, count, receive_back, 0)

    def widen(source, carry):
        start_ref[pl.ds(source * piece, piece), :] = entering[source].astype(jnp.float32)
        return carry

    lax.fori_loop(0, count, widen, 0)

    def second(turn, carry):
        first = turn * pair
        for lead in range(0, states, span):
            begin = [lines(start_ref, first + g, lead + n, states) for g in range(pair) for n in range(span)]
            sweep(first, lead, begin, True)
        return carry

    lax.fori_loop(0, groups // pair, second, 0)

    def out_tile(position, carry):
        lanes = pl.ds(pl.multiple_of(position * LANES, LANES), LANES)
        rows = pl.ds(pl.multiple_of(position * length, length), length)
        result = sums[rows, :] + gain_ref[:, lanes] * conv_ref[rows, :]
        mixed_ref[:, lanes] = (result * silu(z_ref[:, lanes].astype(jnp.float32))).astype(jnp.bfloat16)
        return carry

    lax.fori_loop(0, tiles, out_tile, 0)

    @pl.when(me < count - 1)
    def _():
        rim_copy.wait_send()

    pass_on(me, True, True, sent)
    for hop in range(1, planes):
        column_step(hop, sent, False)
    for hop in range(planes):
        across_step(hop, sent, False)


def hand_out(mixed_ref, hidden_ref, mixed_out, hidden_out, sems):
    copies = []
    for source, target in ((mixed_ref, mixed_out), (hidden_ref, hidden_out)):
        share = source.shape[0] // 4
        for part in range(4):
            rows = pl.ds(part * share, share)
            copies.append(pltpu.make_async_copy(source.at[rows, :], target.at[rows, :], sems.at[len(copies)]))
    for copy in copies:
        copy.start()
    for copy in copies:
        copy.wait()


def shards(
    inner_x,
    inner_z,
    step_raw,
    conv_weight,
    state_proj,
    step_bias,
    decay_log,
    skip_gain,
    moe_tokens,
    routes,
    gate_weight,
    up_weight,
):
    length, channels = inner_x.shape
    states = decay_log.shape[0]
    count, flight = lax.axis_size("seq"), lax.axis_size("exp")
    hidden_rows, features = gate_weight.shape[1:]
    width = moe_tokens.shape[1]
    tiles = channels // LANES
    piece = tiles * states // count
    spread = max(1, piece // states)
    slots = CAP * count
    whole, half = jnp.float32, jnp.bfloat16
    flat = pltpu.VMEM((tiles * length, LANES), whole)
    table = pltpu.VMEM((states * length, LANES), whole)
    held = pltpu.VMEM((tiles * states, LANES), whole)
    pieces = pltpu.VMEM((count, piece, LANES), half)
    ends = pltpu.VMEM((count, -(-piece // 16) * 16 + -(-3 * spread // 16) * 16, LANES), half)
    block = (16, width + width // 4)
    dma = pltpu.SemaphoreType.DMA
    in_vmem = pl.BlockSpec(memory_space=pltpu.VMEM)
    in_hbm = pl.BlockSpec(memory_space=pltpu.HBM)
    operands = (
        inner_x, inner_z, step_raw, conv_weight, state_proj.T, step_bias[None, :], decay_log, skip_gain[None, :],
        moe_tokens, routes.T,
    )
    mixed, hidden = pl.pallas_call(
        functools.partial(mixer_kernel, count, flight),
        out_shape=(
            jax.ShapeDtypeStruct((length, channels), half),
            jax.ShapeDtypeStruct((slots, hidden_rows), half),
        ),
        in_specs=[in_hbm] * 12,
        out_specs=(in_vmem, in_vmem),
        scratch_shapes=[
            *(pltpu.VMEM(operand.shape, operand.dtype) for operand in operands),
            pltpu.VMEM((hidden_rows, features), half),
            pltpu.VMEM((hidden_rows, features), half),
            pltpu.VMEM((16, channels), half),
            pltpu.VMEM((length + 16, LANES), whole),
            pltpu.VMEM((length, channels), half),
            flat,
            flat,
            flat,
            pltpu.VMEM((flight, length, 2 * states), whole),
            pltpu.VMEM((length, 2 * states), whole),
            table,
            table,
            held,
            held,
            pltpu.VMEM((tiles, LANES), whole),
            ends,
            ends,
            pieces,
            pieces,
            held,
            flat,
            pltpu.VMEM((flight, *block), half),
            pltpu.VMEM((count, flight, *block), half),
            pltpu.VMEM((slots, features), half),
            pltpu.VMEM((slots, slots), half),
            dma((12,)),
            dma((2,)),
            dma((2, flight)),
            dma((2, flight)),
            dma((4, count)),
            dma((count,)),
            dma((2, count)),
            dma((2, count)),
        ],
        compiler_params=pltpu.CompilerParams(
            vmem_limit_bytes=VMEM_LIMIT, collective_id=0, has_side_effects=True
        ),
    )(*operands, gate_weight[0], up_weight[0])
    mixed, hidden = pl.pallas_call(
        hand_out,
        out_shape=(
            jax.ShapeDtypeStruct((length, channels), half),
            jax.ShapeDtypeStruct((slots, hidden_rows), half),
        ),
        in_specs=[in_hbm] * 2,
        out_specs=(in_hbm, in_hbm),
        scratch_shapes=[dma((8,))],
        compiler_params=pltpu.CompilerParams(vmem_limit_bytes=VMEM_LIMIT),
    )(mixed, hidden)
    return (mixed, hidden.T[None])


def solution(mesh):
    return jax.shard_map(
        shards,
        mesh=mesh,
        in_specs=(
            P("seq", "exp"),
            P("seq", "exp"),
            P("seq", "exp"),
            P(None, "exp"),
            P("exp", None),
            P("exp"),
            P(None, "exp"),
            P("exp"),
            P("seq", "exp"),
            P("seq", None),
            P("exp", "seq", None),
            P("exp", "seq", None),
        ),
        out_specs=(P("seq", "exp"), P("exp", "seq", None)),
        check_vma=False,
    )
```

```python
import functools

import jax
import jax.numpy as jnp
from jax import lax
from jax.experimental import pallas as pl
from jax.experimental.pallas import tpu as pltpu
from jax.sharding import PartitionSpec as P

CAP = 20
TURN = 8
LANES = 128
SUB = 8
LOG2E = 1.4426950408889634
MESH = pl.DeviceIdType.MESH
VMEM_LIMIT = 60 * 1024 * 1024


def silu(value):
    half = 0.5 * value
    return half + half * jnp.tanh(half)


def softplus(value):
    grown = jnp.exp(value)
    series = grown * (1.0 - grown * (0.5 - grown * (1.0 / 3.0 - 0.25 * grown)))
    return jnp.where(grown < 0.03, series, jnp.log(1.0 + grown))


def splat_columns(coef_ref, first, count, table):
    length = coef_ref.shape[0]
    for column in range(count):
        table[pl.ds(column * length, length), :] = jnp.broadcast_to(
            coef_ref[:, first + column : first + column + 1], (length, LANES)
        )


def rate_rows(decay_ref, table):
    states, channels = decay_ref.shape

    def tile(position, carry):
        lanes = pl.ds(pl.multiple_of(position * LANES, LANES), LANES)
        rows = pl.ds(pl.multiple_of(position * states, states), states)
        table[rows, :] = jnp.exp(decay_ref[:, lanes]) * (-LOG2E)
        return carry

    lax.fori_loop(0, channels // LANES, tile, 0)


def mixer_kernel(
    count, flight, x_hbm, z_hbm, raw_hbm, taps_hbm, proj_hbm, bias_hbm, decay_hbm, gain_hbm, tokens_hbm, routes_hbm,
    gate_hbm, up_hbm, mixed_ref, hidden_ref,
    x_ref, z_ref, raw_ref, taps_ref, proj_ref, bias_ref, decay_ref, gain_ref, tokens_ref, routes_ref,
    gate_ref, up_ref, rim_ref, wide, rounded, conv_ref, step_ref, drive_ref, parts_ref, coef_ref, in_table, out_table,
    rate_ref, end_ref, total_ref, end_out, got_end, leaving, entering, start_ref, sums,
    stage, block_rows, rows_ref, order_ref,
    local_sem, rim_sem, pair_out, pair_in, rows_out, rows_in, sends, arrivals,
):
    length, channels = x_ref.shape
    states = decay_ref.shape[0]
    taps = taps_ref.shape[0]
    width = tokens_ref.shape[1]
    quarter = width // 4
    tiles = channels // LANES
    piece = tiles * states // count
    spread = max(1, piece // states)
    lead_rows = -(-piece // 16) * 16
    extra_rows = end_out.shape[1] - lead_rows
    hidden_rows = gate_ref.shape[0]
    chunk = 256 if hidden_rows % 256 == 0 else hidden_rows
    me, side = lax.axis_index("seq"), lax.axis_index("exp")

    def seq_peer(distance):
        return lax.rem(me + distance, count)

    def exp_peer(distance):
        return lax.rem(side + distance, flight)

    loads = [
        pltpu.make_async_copy(source, target, local_sem.at[number])
        for number, (source, target) in enumerate(
            (
                (routes_hbm, routes_ref), (tokens_hbm, tokens_ref), (raw_hbm, raw_ref), (bias_hbm, bias_ref),
                (decay_hbm, decay_ref), (x_hbm, x_ref), (taps_hbm, taps_ref), (proj_hbm, proj_ref),
                (z_hbm, z_ref), (gain_hbm, gain_ref), (gate_hbm, gate_ref), (up_hbm, up_ref),
            )
        )
    ]
    for load in loads:
        load.start()

    barrier = pltpu.get_barrier_semaphore()

    def greet(distance, carry):
        pl.semaphore_signal(barrier, inc=1, device_id=(seq_peer(distance), side), device_id_type=MESH)
        return carry

    lax.fori_loop(1, count, greet, 0)
    for distance in range(1, flight):
        pl.semaphore_signal(barrier, inc=1, device_id=(me, exp_peer(distance)), device_id_type=MESH)
    pl.semaphore_wait(barrier, count - 1 + flight - 1)

    def remote(source, target, send_sem, arrive_sem, seq_index, exp_index):
        return pltpu.make_async_remote_copy(
            source, target, send_sem, arrive_sem, device_id=(seq_index, exp_index), device_id_type=MESH
        )

    rim_copy = remote(
        x_hbm.at[pl.ds(length - 16, 16), :], rim_ref, rim_sem.at[0], rim_sem.at[1], seq_peer(1), side
    )

    @pl.when(me < count - 1)
    def _():
        rim_copy.start()

    above = lax.broadcasted_iota(jnp.int32, (length, length), 0) < lax.broadcasted_iota(
        jnp.int32, (length, length), 1
    )
    above = above.astype(jnp.float32).astype(jnp.bfloat16)
    slot = lax.broadcasted_iota(jnp.int32, (16, length), 0)
    for load in loads[:2]:
        load.wait()
    for expert in range(flight):
        named = (routes_ref[pl.ds(0, 1), :] == expert).astype(jnp.float32)
        for choice in range(1, routes_ref.shape[0]):
            named = named + (routes_ref[pl.ds(choice, 1), :] == expert).astype(jnp.float32)
        named = jnp.broadcast_to(named, (16, length))
        rank = jnp.dot(named.astype(jnp.bfloat16), above, preferred_element_type=jnp.float32)
        taken = jnp.where(rank == slot.astype(jnp.float32), named, 0.0).astype(jnp.bfloat16)
        stage[expert, :, pl.ds(0, width)] = jnp.dot(
            taken, tokens_ref[...], preferred_element_type=jnp.float32
        ).astype(jnp.bfloat16)
        late = jnp.where(rank == (16 + (slot & 3)).astype(jnp.float32), named, 0.0)
        rest = jnp.zeros((16, quarter), jnp.float32)
        for part in range(4):
            mine = jnp.where((slot >> 2) == part, late, 0.0).astype(jnp.bfloat16)
            rest = rest + jnp.dot(
                mine, tokens_ref[:, pl.ds(part * quarter, quarter)], preferred_element_type=jnp.float32
            )
        stage[expert, :, pl.ds(width, quarter)] = rest.astype(jnp.bfloat16)

    def stage_copy(distance):
        return remote(
            stage.at[exp_peer(distance)], block_rows.at[me, side],
            pair_out.at[0, distance], pair_in.at[0, distance], me, exp_peer(distance),
        )

    def coef_copy(distance):
        return remote(
            parts_ref.at[side], parts_ref.at[side],
            pair_out.at[1, distance], pair_in.at[1, distance], me, exp_peer(distance),
        )

    for distance in range(1, flight):
        stage_copy(distance).start()
    block_rows[me, side] = stage[side]

    def step_tile(position, carry):
        lanes = pl.ds(pl.multiple_of(position * LANES, LANES), LANES)
        rows = pl.ds(pl.multiple_of(position * length, length), length)
        step_ref[rows, :] = softplus(raw_ref[:, lanes].astype(jnp.float32) + bias_ref[:, lanes])
        return carry

    for load in loads[2:4]:
        load.wait()
    lax.fori_loop(0, tiles // 2, step_tile, 0)

    low = lax.rem(me, 4)
    plane = me // 4
    planes = count // 4
    across = me - low + lax.rem(low + 2, 4)
    beside = me + 1 - 2 * lax.rem(me, 2)
    far = across + 1 - 2 * lax.rem(across, 2)

    def row_copy(kind, source):
        target = (me + 4, me - 4, across, beside)[kind]
        return remote(
            block_rows.at[source], block_rows.at[source], rows_out.at[kind, source], rows_in.at[source], target, side
        )

    def arrived(source):
        row_copy(3, source).wait_recv()

    def pass_on(source, up, down, act):
        if up:
            pl.when(plane < planes - 1)(lambda: act(row_copy(0, source)))
        if down:
            pl.when(plane > 0)(lambda: act(row_copy(1, source)))
        act(row_copy(2, source))
        act(row_copy(3, source))

    def column_step(hop, act, wait):
        @pl.when(plane >= hop)
        def _():
            if wait:
                arrived(me - 4 * hop)
            pass_on(me - 4 * hop, True, False, act)

        @pl.when(plane + hop < planes)
        def _():
            if wait:
                arrived(me + 4 * hop)
            pass_on(me + 4 * hop, False, True, act)

    def across_step(hop, act, wait):
        if hop == 0:
            if wait:
                arrived(across)
            act(row_copy(3, across))
            return

        @pl.when(plane >= hop)
        def _():
            if wait:
                arrived(across - 4 * hop)
            act(row_copy(3, across - 4 * hop))

        @pl.when(plane + hop < planes)
        def _():
            if wait:
                arrived(across + 4 * hop)
            act(row_copy(3, across + 4 * hop))

    def start(copy):
        copy.start()

    def sent(copy):
        copy.wait_send()

    for distance in range(1, flight):
        stage_copy(distance).wait()
    pass_on(me, True, True, start)
    lax.fori_loop(tiles // 2, tiles, step_tile, 0)
    loads[4].wait()
    rate_rows(decay_ref, rate_ref)
    held_at = lax.broadcasted_iota(jnp.int32, order_ref.shape, 1)
    wanted = lax.broadcasted_iota(jnp.int32, order_ref.shape, 0)
    tail_at = held_at - 16 * count
    goes_to = jnp.where(
        held_at < 16 * count,
        (held_at >> 4) * CAP + (held_at & 15),
        (tail_at >> 2) * CAP + 16 + (tail_at & 3),
    )
    order_ref[...] = (goes_to == wanted).astype(jnp.float32).astype(jnp.bfloat16)
    for load in loads[5:8]:
        load.wait()

    @pl.when(me > 0)
    def _():
        rim_copy.wait_recv()

    @pl.when(me == 0)
    def _():
        rim_ref[...] = jnp.zeros_like(rim_ref)

    def conv_tile(position, carry):
        lanes = pl.ds(pl.multiple_of(position * LANES, LANES), LANES)
        rows = pl.ds(pl.multiple_of(position * length, length), length)
        wide[pl.ds(0, 16), :] = rim_ref[:, lanes].astype(jnp.float32)
        wide[pl.ds(16, length), :] = x_ref[:, lanes].astype(jnp.float32)
        total = taps_ref[pl.ds(0, 1), lanes] * wide[pl.ds(17 - taps, length), :]
        for tap in range(1, taps):
            total = total + taps_ref[pl.ds(tap, 1), lanes] * wide[pl.ds(17 - taps + tap, length), :]
        conv = silu(total)
        conv_ref[rows, :] = conv
        drive_ref[rows, :] = step_ref[rows, :] * conv
        rounded[:, lanes] = conv.astype(jnp.bfloat16)
        return carry

    lax.fori_loop(0, tiles // 2, conv_tile, 0)
    if planes > 1:
        column_step(1, start, True)
    lax.fori_loop(tiles // 2, tiles, conv_tile, 0)
    dims = (((1,), (1,)), ((), ()))
    parts_ref[side] = lax.dot_general(rounded[...], proj_ref[...], dims, preferred_element_type=jnp.float32)
    for distance in range(1, flight):
        coef_copy(distance).start()
    if planes > 2:
        column_step(2, start, True)
    for distance in range(1, flight):
        coef_copy(distance).wait()
    coef = parts_ref[0]
    for other in range(1, flight):
        coef = coef + parts_ref[other]
    coef_ref[...] = coef
    splat_columns(coef_ref, 0, states, in_table)
    splat_columns(coef_ref, states, states, out_table)

    groups = tiles // SUB
    pair = 2 if groups % 2 == 0 else 1
    span = states // pair

    def lines(ref, group, offset, stride):
        return ref[pl.ds(group * SUB * stride + offset, SUB, stride=stride), :]

    def sweep(first, lead, begin, output):
        rates = [[lines(rate_ref, first + g, lead + n, states) for n in range(span)] for g in range(pair)]
        keep_total = lead == 0 and not output

        def block(turn, held):
            state = [list(held[g * span : (g + 1) * span]) for g in range(pair)]
            totals = list(held[pair * span :])
            for inner in range(TURN):
                t = turn * TURN + inner
                steps = [lines(step_ref, first + g, t, length) for g in range(pair)]
                drives = [lines(drive_ref, first + g, t, length) for g in range(pair)]
                if keep_total:
                    totals = [totals[g] + steps[g] for g in range(pair)]
                terms = [[None, None] for _ in range(pair)]
                for n in range(span):
                    row = in_table[pl.ds((lead + n) * length + t, 1), :]
                    if output:
                        out_row = out_table[pl.ds((lead + n) * length + t, 1), :]
                    for g in range(pair):
                        state[g][n] = jnp.exp2(rates[g][n] * steps[g]) * state[g][n] + row * drives[g]
                        if output:
                            term = out_row * state[g][n]
                            old = terms[g][n % 2]
                            terms[g][n % 2] = term if old is None else old + term
                if output:
                    for g in range(pair):
                        where = pl.ds((first + g) * SUB * length + t, SUB, stride=length)
                        part = terms[g][0] if span == 1 else terms[g][0] + terms[g][1]
                        sums[where, :] = part if lead == 0 else sums[where, :] + part
            return tuple(s for line in state for s in line) + tuple(totals)

        zeros = (jnp.zeros((SUB, LANES), jnp.float32),) * (pair if keep_total else 0)
        held = lax.fori_loop(0, length // TURN, block, tuple(begin) + zeros)
        if keep_total:
            for g in range(pair):
                total_ref[pl.ds(pl.multiple_of((first + g) * SUB, SUB), SUB), :] = held[pair * span + g]
        return held

    def carry_copy(kind, distance):
        peer = seq_peer(distance)
        source = (end_out.at[peer], leaving.at[peer])[kind]
        target = (got_end.at[me], entering.at[me])[kind]
        return remote(source, target, sends.at[kind, distance], arrivals.at[kind, distance], peer, side)

    def send_ends(begin, stop):
        def one(peer, carry):
            end_out[peer, pl.ds(0, piece), :] = end_ref[pl.ds(peer * piece, piece), :].astype(jnp.bfloat16)
            line = lax.broadcasted_iota(jnp.int32, (extra_rows, LANES), 0)
            rest = jnp.zeros((extra_rows, LANES), jnp.float32)
            for row in range(spread):
                total = total_ref[pl.ds(peer * piece // states + row, 1), :]
                for part in range(3):
                    top = total.astype(jnp.bfloat16).astype(jnp.float32)
                    rest = jnp.where(line == part * spread + row, top, rest)
                    total = total - top
            end_out[peer, pl.ds(lead_rows, extra_rows), :] = rest.astype(jnp.bfloat16)

            @pl.when(peer != me)
            def _():
                distance = lax.rem(peer - me + count, count)
                carry_copy(0, distance).start()

            return carry

        lax.fori_loop(begin, stop, one, 0)

    events = [lambda hop=hop: column_step(hop, start, True) for hop in range(3, planes)]
    events += [lambda hop=hop: across_step(hop, start, True) for hop in range(planes)]
    units = [(first, lead) for first in range(0, groups, pair) for lead in range(0, states, span)]
    for number, (first, lead) in enumerate(units):
        zero = jnp.zeros((SUB, LANES), jnp.float32)
        held = sweep(first, lead, (zero,) * (pair * span), False)
        for g in range(pair):
            for n in range(span):
                end_ref[pl.ds((first + g) * SUB * states + lead + n, SUB, stride=states), :] = held[g * span + n]
        if lead + span == states:
            send_ends(count * first // groups, count * (first + pair) // groups)
        for _ in range(0 if number == len(units) - 1 else min(len(events), 1 + (number == 0))):
            events.pop(0)()
    got_end[me] = end_out[me]
    for event in events:
        event()

    def last_rows(turn, carry):
        arrived(lax.rem(beside, 4) + 4 * turn)
        arrived(lax.rem(far, 4) + 4 * turn)
        return carry

    lax.fori_loop(0, planes, last_rows, 0)

    small = 4 * count
    for half in range(flight):
        def lay_rows(source, carry):
            rows_ref[pl.ds(pl.multiple_of(source * 16, 16), 16), pl.ds(half * width, width)] = block_rows[
                source, half, :, pl.ds(0, width)
            ]
            return carry

        lax.fori_loop(0, count, lay_rows, 0)
        rest = block_rows[:, half, :, pl.ds(width, quarter)].reshape(16 * count, quarter)
        into = lax.broadcasted_iota(jnp.int32, (small, 16 * count), 0)
        out_of = lax.broadcasted_iota(jnp.int32, (small, 16 * count), 1)
        for part in range(4):
            pick = ((into >> 2) * 16 + part * 4 + (into & 3) == out_of).astype(jnp.float32).astype(jnp.bfloat16)
            rows_ref[pl.ds(16 * count, small), pl.ds(half * width + part * quarter, quarter)] = jnp.dot(
                pick, rest, preferred_element_type=jnp.float32
            ).astype(jnp.bfloat16)
    def receive(distance, carry):
        carry_copy(0, distance).wait()
        return carry

    lax.fori_loop(1, count, receive, 0)
    own_rates = rate_ref[pl.ds(me * piece, piece), :]

    column = lax.broadcasted_iota(jnp.int32, (piece, extra_rows), 1)
    kept = lax.broadcasted_iota(jnp.int32, (piece, extra_rows), 0) // (piece // spread)
    adds = jnp.zeros((piece, extra_rows), jnp.float32)
    for part in range(3):
        adds = adds + (column == part * spread + kept).astype(jnp.float32)
    adds = adds.astype(jnp.bfloat16)

    def join(source, state):
        leaving[source] = state.astype(jnp.bfloat16)

        @pl.when(source != me)
        def _():
            carry_copy(1, lax.rem(source - me + count, count)).start()

        totals = jnp.dot(
            adds, got_end[source, pl.ds(lead_rows, extra_rows), :], preferred_element_type=jnp.float32
        )
        return jnp.exp2(own_rates * totals) * state + got_end[source, pl.ds(0, piece), :].astype(jnp.float32)

    lax.fori_loop(0, count, join, jnp.zeros((piece, LANES), jnp.float32), unroll=4)
    entering[me] = leaving[me]
    for load in loads[8:]:
        load.wait()
    for turn in range(hidden_rows // chunk):
        part = pl.ds(turn * chunk, chunk)
        gate = lax.dot_general(rows_ref[...], gate_ref[part, :], dims, preferred_element_type=jnp.float32)
        up = lax.dot_general(rows_ref[...], up_ref[part, :], dims, preferred_element_type=jnp.float32)
        value = (silu(gate) * up).astype(jnp.bfloat16)
        hidden_ref[:, part] = jnp.dot(order_ref[...], value, preferred_element_type=jnp.float32).astype(
            jnp.bfloat16
        )

    def receive_back(distance, carry):
        carry_copy(1, distance).wait()
        return carry

    lax.fori_loop(1, count, receive_back, 0)

    def widen(source, carry):
        start_ref[pl.ds(source * piece, piece), :] = entering[source].astype(jnp.float32)
        return carry

    lax.fori_loop(0, count, widen, 0)

    def second(turn, carry):
        first = turn * pair
        for lead in range(0, states, span):
            begin = [lines(start_ref, first + g, lead + n, states) for g in range(pair) for n in range(span)]
            sweep(first, lead, begin, True)
        return carry

    lax.fori_loop(0, groups // pair, second, 0)

    def out_tile(position, carry):
        lanes = pl.ds(pl.multiple_of(position * LANES, LANES), LANES)
        rows = pl.ds(pl.multiple_of(position * length, length), length)
        result = sums[rows, :] + gain_ref[:, lanes] * conv_ref[rows, :]
        mixed_ref[:, lanes] = (result * silu(z_ref[:, lanes].astype(jnp.float32))).astype(jnp.bfloat16)
        return carry

    lax.fori_loop(0, tiles, out_tile, 0)

    @pl.when(me < count - 1)
    def _():
        rim_copy.wait_send()

    pass_on(me, True, True, sent)
    for hop in range(1, planes):
        column_step(hop, sent, False)
    for hop in range(planes):
        across_step(hop, sent, False)


def hand_out(mixed_ref, hidden_ref, mixed_out, hidden_out):
    mixed_out[...] = mixed_ref[...]
    hidden_out[...] = hidden_ref[...]


def shards(
    inner_x,
    inner_z,
    step_raw,
    conv_weight,
    state_proj,
    step_bias,
    decay_log,
    skip_gain,
    moe_tokens,
    routes,
    gate_weight,
    up_weight,
):
    length, channels = inner_x.shape
    states = decay_log.shape[0]
    count, flight = lax.axis_size("seq"), lax.axis_size("exp")
    hidden_rows, features = gate_weight.shape[1:]
    width = moe_tokens.shape[1]
    tiles = channels // LANES
    piece = tiles * states // count
    spread = max(1, piece // states)
    slots = CAP * count
    whole, half = jnp.float32, jnp.bfloat16
    flat = pltpu.VMEM((tiles * length, LANES), whole)
    table = pltpu.VMEM((states * length, LANES), whole)
    held = pltpu.VMEM((tiles * states, LANES), whole)
    pieces = pltpu.VMEM((count, piece, LANES), half)
    ends = pltpu.VMEM((count, -(-piece // 16) * 16 + -(-3 * spread // 16) * 16, LANES), half)
    block = (16, width + width // 4)
    dma = pltpu.SemaphoreType.DMA
    in_vmem = pl.BlockSpec(memory_space=pltpu.VMEM)
    in_hbm = pl.BlockSpec(memory_space=pltpu.HBM)
    operands = (
        inner_x, inner_z, step_raw, conv_weight, state_proj.T, step_bias[None, :], decay_log, skip_gain[None, :],
        moe_tokens, routes.T,
    )
    mixed, hidden = pl.pallas_call(
        functools.partial(mixer_kernel, count, flight),
        out_shape=(
            jax.ShapeDtypeStruct((length, channels), half),
            jax.ShapeDtypeStruct((slots, hidden_rows), half),
        ),
        in_specs=[in_hbm] * 12,
        out_specs=(in_vmem, in_vmem),
        scratch_shapes=[
            *(pltpu.VMEM(operand.shape, operand.dtype) for operand in operands),
            pltpu.VMEM((hidden_rows, features), half),
            pltpu.VMEM((hidden_rows, features), half),
            pltpu.VMEM((16, channels), half),
            pltpu.VMEM((length + 16, LANES), whole),
            pltpu.VMEM((length, channels), half),
            flat,
            flat,
            flat,
            pltpu.VMEM((flight, length, 2 * states), whole),
            pltpu.VMEM((length, 2 * states), whole),
            table,
            table,
            held,
            held,
            pltpu.VMEM((tiles, LANES), whole),
            ends,
            ends,
            pieces,
            pieces,
            held,
            flat,
            pltpu.VMEM((flight, *block), half),
            pltpu.VMEM((count, flight, *block), half),
            pltpu.VMEM((slots, features), half),
            pltpu.VMEM((slots, slots), half),
            dma((12,)),
            dma((2,)),
            dma((2, flight)),
            dma((2, flight)),
            dma((4, count)),
            dma((count,)),
            dma((2, count)),
            dma((2, count)),
        ],
        compiler_params=pltpu.CompilerParams(
            vmem_limit_bytes=VMEM_LIMIT, collective_id=0, has_side_effects=True
        ),
    )(*operands, gate_weight[0], up_weight[0])
    strips = [
        pl.BlockSpec((length // 4, channels), lambda turn: (turn, 0)),
        pl.BlockSpec((slots // 4, hidden_rows), lambda turn: (turn, 0)),
    ]
    mixed, hidden = pl.pallas_call(
        hand_out,
        out_shape=(
            jax.ShapeDtypeStruct((length, channels), half),
            jax.ShapeDtypeStruct((slots, hidden_rows), half),
        ),
        grid=(4,),
        in_specs=strips,
        out_specs=tuple(strips),
        compiler_params=pltpu.CompilerParams(vmem_limit_bytes=VMEM_LIMIT),
    )(mixed, hidden)
    return (mixed, hidden.T[None])


def solution(mesh):
    return jax.shard_map(
        shards,
        mesh=mesh,
        in_specs=(
            P("seq", "exp"),
            P("seq", "exp"),
            P("seq", "exp"),
            P(None, "exp"),
            P("exp", None),
            P("exp"),
            P(None, "exp"),
            P("exp"),
            P("seq", "exp"),
            P("seq", None),
            P("exp", "seq", None),
            P("exp", "seq", None),
        ),
        out_specs=(P("seq", "exp"), P("exp", "seq", None)),
        check_vma=False,
    )
```
